256 devices in a mesh: dp: 8 (over x_hi, y), feat: 32 (over z, x_lo, core).
Axes of the slice: x: 4 (x_hi: 2, x_lo: 2; x = x_hi * 2 + x_lo), y: 4, z: 8, core: 2. Of those that a mesh axis runs over, the one named last changes fastest.
Arguments:
- view_a: bfloat16 [3072, 1536], P('dp'), may hold values from -24 to 24
- view_b: bfloat16 [3072, 1536], P('dp'), may hold values from -24 to 24
- proj_weight: bfloat16 [1536, 8192], P(None, 'feat'), may hold values from -0.15625 to 0.15625
Outputs:
- grad_a: float32 [3072, 8192], P('dp', 'feat')
- grad_b: float32 [3072, 8192], P('dp', 'feat')
The draws below stay inside these ranges and needn't reach their ends.
All inputs are finite; a program needn't handle non-finite values.
Results may differ from the reference program's by a relative error of at most 0.0023.
Values may be sent and summed in bfloat16 or wider, within the bound.
No kernel may reach another device: no remote copies, remote signals or barrier semaphores. Data moves between devices by JAX's collectives and lax.ppermute only.
A program may use at most 128 MiB of HBM per device.

```python
import jax
import jax.numpy as jnp
from jax import lax

K = 1536
F = 8192
ROWS = 384
TOTAL = 3072
N_DP = 8


def shared_views(key):
    base = jnp.clip(jax.random.normal(jax.random.fold_in(key, 11), (TOTAL, K), jnp.float32), -5.0, 5.0)
    noise = jnp.clip(jax.random.normal(jax.random.fold_in(key, 12), (TOTAL, K), jnp.float32), -5.0, 5.0)
    return (base, noise)


def draw_view_a(key, part):
    base, noise = shared_views(key)
    return base.astype(jnp.bfloat16)


def draw_view_b(key, part):
    base, noise = shared_views(key)
    return (0.9 * base + 0.436 * noise).astype(jnp.bfloat16)


def steps_of(key, extent, split, low, top_value):
    def one(dim, blocks):
        steps = jax.random.uniform(jax.random.fold_in(jax.random.fold_in(key, 6), dim), (blocks,), jnp.float32, low / len(split), top_value / len(split))
        return jnp.repeat(jnp.exp(steps), extent[dim] // blocks).reshape((-1,) + (1,) * (len(extent) - dim - 1))

    loudness = one(*split[0])
    for cut in split[1:]:
        loudness = loudness * one(*cut)
    return loudness


def centred(own_key, shape, deviation, limit, split=(), held_as=jnp.bfloat16):
    result = deviation * jax.random.normal(own_key, shape, jnp.float32)
    if split:
        result = result * steps_of(own_key, shape, split, -0.22, 0.18)
    return jnp.clip(result, -limit, limit).astype(held_as)


def setup_inputs(seed: int = 0) -> dict:
    splits = jax.random.split(jax.random.key(seed), 4)
    return {
        "view_a": draw_view_a(jax.random.fold_in(splits[3], 71), 0),
        "view_b": draw_view_b(jax.random.fold_in(splits[3], 71), 0),
        "proj_weight": centred(splits[2], (K, F), K ** -0.5, 0.15625, ((1, 32),)),
    }


off_weight = 0.5

def reference(view_a, view_b, proj_weight):
    proj_a = jnp.dot(view_a, proj_weight, preferred_element_type=jnp.float32)
    proj_b = jnp.dot(view_b, proj_weight, preferred_element_type=jnp.float32)

    def normalize(proj):
        mean = lax.optimization_barrier(jnp.sum(proj, axis=0)) / TOTAL
        var = lax.optimization_barrier(jnp.sum(proj * proj, axis=0)) / TOTAL - mean * mean
        return ((proj - mean) * lax.rsqrt(var + 1e-05)).astype(jnp.bfloat16)
    norm_a = normalize(proj_a)
    norm_b = normalize(proj_b)
    blocks_a = norm_a.reshape(N_DP, ROWS, F)
    blocks_b = norm_b.reshape(N_DP, ROWS, F)

    def add_block(total, pair):
        block_a, block_b = pair
        term = lax.dot_general(block_a, block_b, (((0,), (0,)), ((), ())), preferred_element_type=jnp.float32) / TOTAL
        return (total + term, None)
    cross, unused = lax.scan(add_block, jnp.zeros((F, F), jnp.float32), (blocks_a, blocks_b))
    diag_mask = jnp.arange(F, dtype=jnp.int32)[:, None] == jnp.arange(F, dtype=jnp.int32)[None, :]
    grad_c = jnp.where(diag_mask, -2.0 * (1.0 - cross), 2.0 * off_weight * cross).astype(jnp.bfloat16)
    grad_a = lax.dot_general(norm_b, grad_c, (((1,), (1,)), ((), ())), preferred_element_type=jnp.float32)
    grad_b = jnp.dot(norm_a, grad_c, preferred_element_type=jnp.float32)
    return (grad_a, grad_b)
```

```python
import jax
import jax.numpy as jnp
import numpy as np
from jax import lax
from jax.experimental import pallas as pl
from jax.experimental.pallas import tpu as pltpu
from jax.sharding import Mesh, PartitionSpec as P

DP = ("xh", "y")
FEAT = ("z", "xl", "c")
PARTS = {"xh": 2, "y": 4, "z": 8, "xl": 2, "c": 2}
SWAP = [(0, 1), (1, 0)]
U_SCALE = 1024.0
EPS = 1e-05
f32, bf16, f16 = jnp.float32, jnp.bfloat16, jnp.float16

ROWS = 384
TOTAL = 3072
DEPTH = 1536
BLOCK = 256
QUARTER = ROWS // 4
PIECE = (48, 768)
SHARE = DEPTH // 4
VMEM = pl.BlockSpec(memory_space=pltpu.VMEM)
SMEM = pl.BlockSpec(memory_space=pltpu.SMEM)


def exchange(blocks, axes):
    return lax.all_to_all(blocks, axes, split_axis=0, concat_axis=0, tiled=True)


def dot(a, b, ca, cb):
    return lax.dot_general(a, b, (((ca,), (cb,)), ((), ())), preferred_element_type=f32)


def call(body, out, n_in, flops, nbytes, scratch=(), smem=False, name=None, vmem=60):
    return pl.pallas_call(
        body,
        out_shape=out,
        in_specs=([SMEM] if smem else []) + [VMEM] * n_in,
        out_specs=jax.tree.map(lambda _: VMEM, out),
        scratch_shapes=scratch,
        compiler_params=pltpu.CompilerParams(vmem_limit_bytes=vmem * 2**20),
        cost_estimate=pl.CostEstimate(flops=flops, bytes_accessed=nbytes, transcendentals=0),
        name=name,
    )


def project(va, vb, w, pa, pb, sums):
    a = dot(va[...], w[...], 1, 0)
    b = dot(vb[...], w[...], 1, 0)
    pa[...] = a
    pb[...] = b
    col = [jnp.sum(t, axis=0, keepdims=True) for t in (a, a * a, b, b * b, a * b)]
    own = jnp.concatenate(col + [jnp.zeros((3, BLOCK), f32)], axis=0)
    sums[...] = jnp.broadcast_to(own[None], sums.shape)


def moments(sums, q):
    t = sums[q]
    for d in range(1, 8):
        t = t + sums[4 * d + q]
    t = t * (1.0 / TOTAL)
    ma, mb = t[0:1], t[2:3]
    ra = lax.rsqrt(t[1:2] - ma * ma + EPS)
    rb = lax.rsqrt(t[3:4] - mb * mb + EPS)
    return ma, ra, mb, rb, (t[4:5] - ma * mb) * ra * rb


def embed(place, sums, va, vb, w0, w1, w2, w3, y, na, nb):
    q = place[0]
    at = pl.ds(pl.multiple_of(q * QUARTER, 32), QUARTER)
    v = jnp.concatenate([va[at, :], vb[at, :]], axis=0)
    ws = (w0, w1, w2, w3)
    for j, wj in enumerate(ws):
        ma, ra, mb, rb, _ = moments(sums, q ^ j)
        p = dot(v, wj[...], 1, 0)
        cols = slice(j * BLOCK, (j + 1) * BLOCK)
        na[:, cols] = ((p[:QUARTER] - ma) * (ra * ra)).astype(bf16)
        nb[:, cols] = ((p[QUARTER:] - mb) * (rb * rb)).astype(bf16)
    n = jnp.concatenate([na[...], nb[...]], axis=0)
    for k in range(6):
        rows = slice(k * 256, (k + 1) * 256)
        acc = dot(n[:, :BLOCK], w0[rows, :], 1, 1)
        for j in range(1, 4):
            acc = acc + dot(n[:, j * BLOCK : (j + 1) * BLOCK], ws[j][rows, :], 1, 1)
        acc = acc.astype(bf16)
        for i in range(4):
            y[2 * i + k // 3, :, (k % 3) * 256 : (k % 3 + 1) * 256] = acc[48 * i : 48 * i + 48]


def add_copies(parts, out):
    total = parts[0].astype(f32)
    for d in range(1, 8):
        total = total + parts[d].astype(f32)
    out[...] = jnp.broadcast_to(total.astype(bf16)[None], out.shape)


def turn(va, vb, ta, tb):
    for view, out in ((va, ta), (vb, tb)):
        v = view[...]
        centre = jnp.sum(v.astype(f32), axis=0, keepdims=True) * (1.0 / ROWS)
        centre = jnp.concatenate([centre, jnp.zeros((15, DEPTH), f32)], axis=0).astype(bf16)
        out[...] = jnp.concatenate([v, centre, jnp.zeros((112, DEPTH), bf16)], axis=0).T


def correlate(place, sums, pa, pb, ta, tb, u):
    q, yy = place[0], place[1]
    ma, ra, mb, rb, _ = moments(sums, q)
    for first, p, m, s, t in ((0, pa, ma, ra, tb), (BLOCK, pb, mb, rb, ta)):
        n = (p[...] - m) * s
        rounded = n.astype(bf16)
        excess = jnp.sum(n - rounded.astype(f32), axis=0, keepdims=True)
        excess = jnp.concatenate([excess, jnp.zeros((15, BLOCK), f32)], axis=0).astype(bf16)
        n = jnp.concatenate([rounded, excess, jnp.zeros((112, BLOCK), bf16)], axis=0)
        for b in range(4):
            part = dot(t[b * SHARE : (b + 1) * SHARE, :], n, 1, 0)
            u[b ^ yy, :, first : first + BLOCK] = part * (U_SCALE / TOTAL)


def combine(place, sums, pa, pb, y0, y1, y2, y3, u, out_a, out_b, ya, yb):
    q = place[0]
    for j, yj in enumerate((y0, y1, y2, y3)):
        for i in range(4):
            at = pl.multiple_of((q ^ j) * QUARTER + (i & 1) * 48, 16)
            for h in range(2):
                (ya if i < 2 else yb)[pl.ds(at, 48), h * 768 : (h + 1) * 768] = yj[2 * i + h]
    ma, ra, mb, rb, corr = moments(sums, q)
    for first, y, p, m, s, out in (
        (0, yb, pb, mb, rb, out_a),
        (BLOCK, ya, pa, ma, ra, out_b),
    ):
        acc = (p[...] - m) * (s * (corr - 2.0))
        cols = slice(first, first + BLOCK)
        out[...] = acc + (dot(y[...], u[:DEPTH, cols], 1, 0) + dot(y[...], u[DEPTH:, cols], 1, 0))


def mark(arrived, out):
    out[...] = jnp.zeros(out.shape, f32)


def after(arrived, waiting):
    done = pl.pallas_call(
        mark,
        out_shape=jax.ShapeDtypeStruct((8, 128), f32),
        in_specs=[pl.BlockSpec(memory_space=pl.ANY)],
        out_specs=VMEM,
        cost_estimate=pl.CostEstimate(flops=10**11, bytes_accessed=10**8, transcendentals=0),
        name="mark",
    )(arrived)
    return lax.optimization_barrier((waiting, done))[0]


def split(place, u0, u1, u2, u3, u):
    yy = place[1]
    for s, us in enumerate((u0, u1, u2, u3)):
        x = us[...] * (1.0 / U_SCALE)
        high = x.astype(bf16)
        at = pl.multiple_of((yy ^ s) * SHARE, 128)
        u[pl.ds(at, SHARE), :] = high
        u[pl.ds(DEPTH + at, SHARE), :] = (x - high.astype(f32)).astype(bf16)


def local(va, vb, w):
    q = lax.axis_index("xl") * 2 + lax.axis_index("c")
    place = jnp.stack([q, lax.axis_index("y")]).astype(jnp.int32)
    shape = jax.ShapeDtypeStruct
    tie = lax.optimization_barrier

    w_x = lax.ppermute(w, "xl", SWAP)
    w_c = lax.ppermute(w, "c", SWAP)

    pa, pb, own = call(
        project,
        (shape((ROWS, BLOCK), f32), shape((ROWS, BLOCK), f32), shape((32, 8, BLOCK), f32)),
        3,
        4 * ROWS * DEPTH * BLOCK,
        4 * 2**20,
        name="project",
    )(va, vb, w)
    sums = exchange(own, ("xh", "y", "xl", "c"))
    va_, vb_, _ = tie((va, vb, own))
    ta, tb = call(
        turn, (shape((DEPTH, 512), bf16),) * 2, 2, 10 * 2**20, 6 * 2**20, name="turn"
    )(va_, vb_)
    sums, w_x, w_c, ta, tb = tie((sums, w_x, w_c, ta, tb))
    w_xc = lax.ppermute(w_x, "c", SWAP)

    u_parts = call(
        correlate,
        shape((4, SHARE, 2 * BLOCK), f32),
        5,
        4 * ROWS * DEPTH * BLOCK,
        6 * 2**20,
        smem=True,
        name="correlate",
    )(place, sums, pa, pb, ta, tb)

    def along_y(t, s):
        return lax.ppermute(t, "y", [(i, i ^ s) for i in range(4)])

    u_send = [u_parts[s].astype(f16) for s in (1, 2, 3)]
    sums_, *u_send = tie((sums, *u_send))
    u_recv = [along_y(t, s) for s, t in enumerate(u_send, 1)]

    y_part = call(
        embed,
        shape((8,) + PIECE, bf16),
        7,
        16 * ROWS * DEPTH * BLOCK // 2,
        7 * 2**20,
        [pltpu.VMEM((QUARTER, 4 * BLOCK), bf16)] * 2,
        smem=True,
        name="embed",
    )(place, sums_, va, vb, w, w_c, w_x, w_xc)
    y_parts = exchange(y_part, "z")

    u = u_parts[0]
    for t in u_recv:
        u = u + t.astype(f32)
    u = u.astype(f16)
    u_far = lax.ppermute(u, "xh", SWAP)

    y_parts = after(u, y_parts)
    y_copies = call(
        add_copies, shape((8,) + PIECE, bf16), 1, 10 * 2**20, 2**20, name="add_copies"
    )(y_parts)
    y0 = exchange(y_copies, "z")

    u = (u.astype(f32) + u_far.astype(f32)).astype(f16)
    us = [u] + [along_y(u, s) for s in (1, 2, 3)]
    u = call(
        split,
        shape((2 * DEPTH, 2 * BLOCK), bf16),
        4,
        10**11,
        10**8,
        smem=True,
        name="split",
    )(place, *[t.astype(f32) for t in us])

    y0 = after(u, y0)
    y2 = lax.ppermute(y0, "xl", SWAP)
    y1 = lax.ppermute(y0, "c", SWAP)
    y3 = lax.ppermute(y2, "c", SWAP)

    return call(
        combine,
        (shape((ROWS, BLOCK), f32),) * 2,
        8,
        8 * ROWS * DEPTH * BLOCK,
        8 * 2**20,
        [pltpu.VMEM((ROWS, DEPTH), bf16)] * 2,
        smem=True,
        name="combine",
    )(place, sums, pa, pb, y0, y1, y2, y3, u)


def solution(mesh):
    fine = Mesh(np.asarray(mesh.devices).reshape(tuple(PARTS.values())), tuple(PARTS))
    return jax.shard_map(
        local,
        mesh=fine,
        in_specs=(P(DP, None), P(DP, None), P(None, FEAT)),
        out_specs=(P(DP, FEAT), P(DP, FEAT)),
        check_vma=False,
    )
```

```python
import jax
import jax.numpy as jnp
import numpy as np
from jax import lax
from jax.experimental import pallas as pl
from jax.experimental.pallas import tpu as pltpu
from jax.sharding import Mesh, PartitionSpec as P

DP = ("xh", "y")
FEAT = ("z", "xl", "c")
PARTS = {"xh": 2, "y": 4, "z": 8, "xl": 2, "c": 2}
SWAP = [(0, 1), (1, 0)]
U_SCALE = 1024.0
EPS = 1e-05
f32, bf16, f16 = jnp.float32, jnp.bfloat16, jnp.float16

ROWS = 384
TOTAL = 3072
DEPTH = 1536
BLOCK = 256
QUARTER = ROWS // 4
PIECE = (48, 768)
SHARE = DEPTH // 4
EARLY = 1024
VMEM = pl.BlockSpec(memory_space=pltpu.VMEM)
SMEM = pl.BlockSpec(memory_space=pltpu.SMEM)
ANY = pl.BlockSpec(memory_space=pl.ANY)


def exchange(blocks, axes):
    return lax.all_to_all(blocks, axes, split_axis=0, concat_axis=0, tiled=True)


def dot(a, b, ca, cb):
    return lax.dot_general(a, b, (((ca,), (cb,)), ((), ())), preferred_element_type=f32)


def call(body, out, ins, flops, nbytes, scratch=(), name=None, out_specs=None, vmem=60):
    return pl.pallas_call(
        body,
        out_shape=out,
        in_specs=ins,
        out_specs=out_specs or jax.tree.map(lambda _: VMEM, out),
        scratch_shapes=scratch,
        compiler_params=pltpu.CompilerParams(vmem_limit_bytes=vmem * 2**20),
        cost_estimate=pl.CostEstimate(flops=flops, bytes_accessed=nbytes, transcendentals=0),
        name=name,
    )


def project(va, vb, w, pa, pb, sums, xa, xb, xw, sem):
    third = DEPTH // 3
    copies = []
    for k in range(3):
        at = pl.ds(k * third, third)
        copies.append(
            [
                pltpu.make_async_copy(va.at[:, at], xa.at[k], sem.at[3 * k]),
                pltpu.make_async_copy(vb.at[:, at], xb.at[k], sem.at[3 * k + 1]),
                pltpu.make_async_copy(w.at[at, :], xw.at[k], sem.at[3 * k + 2]),
            ]
        )
    for c in copies:
        for t in c:
            t.start()
    a = b = 0.0
    for k in range(3):
        for t in copies[k]:
            t.wait()
        a = a + dot(xa[k], xw[k], 1, 0)
        b = b + dot(xb[k], xw[k], 1, 0)
    pa[...] = a
    pb[...] = b
    col = [jnp.sum(t, axis=0, keepdims=True) for t in (a, a * a, b, b * b, a * b)]
    own = jnp.concatenate(col + [jnp.zeros((3, BLOCK), f32)], axis=0)
    sums[...] = jnp.broadcast_to(own[None], sums.shape)


def moments(sums, q):
    t = sums[q]
    for d in range(1, 8):
        t = t + sums[4 * d + q]
    t = t * (1.0 / TOTAL)
    ma, mb = t[0:1], t[2:3]
    ra = lax.rsqrt(t[1:2] - ma * ma + EPS)
    rb = lax.rsqrt(t[3:4] - mb * mb + EPS)
    return ma, ra, mb, rb, (t[4:5] - ma * mb) * ra * rb


def embed(place, sums, v, w0, w1, w2, w2b, w3, w3b, y, na, nb):
    q = place[0]
    half = EARLY
    ws = ((w0,), (w1,), (w2, w2b), (w3, w3b))
    for j, wj in enumerate(ws):
        ma, ra, mb, rb, _ = moments(sums, q ^ j)
        if len(wj) == 1:
            p = dot(v[...], wj[0][...], 1, 0)
        else:
            p = dot(v[:, :half], wj[0][...], 1, 0) + dot(v[:, half:], wj[1][...], 1, 0)
        cols = slice(j * BLOCK, (j + 1) * BLOCK)
        na[:, cols] = ((p[:QUARTER] - ma) * (ra * ra)).astype(bf16)
        nb[:, cols] = ((p[QUARTER:] - mb) * (rb * rb)).astype(bf16)
    n = jnp.concatenate([na[...], nb[...]], axis=0)
    for k in range(6):
        acc = 0.0
        for j, wj in enumerate(ws):
            late = len(wj) == 2 and k * 256 >= EARLY
            part = wj[1] if late else wj[0]
            first = k * 256 - (EARLY if late else 0)
            nj = n[:, j * BLOCK : (j + 1) * BLOCK]
            acc = acc + dot(nj, part[first : first + 256, :], 1, 1)
        acc = acc.astype(bf16)
        for i in range(4):
            y[2 * i + k // 3, :, (k % 3) * 256 : (k % 3 + 1) * 256] = acc[48 * i : 48 * i + 48]


def add_copies(parts, ready, out, x, t, sem, out_sem):
    copy = pltpu.make_async_copy(parts, x, sem)
    copy.start()
    copy.wait()
    total = x[0].astype(f32)
    for d in range(1, 8):
        total = total + x[d].astype(f32)
    t[...] = total.astype(bf16)
    done = [pltpu.make_async_copy(t, out.at[d], out_sem.at[d]) for d in range(8)]
    for c in done:
        c.start()
    for c in done:
        c.wait()


def turn(place, va, vb, ta, tb, quarter):
    at = pl.ds(pl.multiple_of(place[0] * QUARTER, 32), QUARTER)
    quarter[:QUARTER] = va[at, :]
    quarter[QUARTER:] = vb[at, :]
    for view, out in ((va, ta), (vb, tb)):
        v = view[...]
        centre = jnp.sum(v.astype(f32), axis=0, keepdims=True) * (1.0 / ROWS)
        centre = jnp.concatenate([centre, jnp.zeros((15, DEPTH), f32)], axis=0).astype(bf16)
        out[...] = jnp.concatenate([v, centre, jnp.zeros((112, DEPTH), bf16)], axis=0).T


def correlate(place, sums, pa, pb, ta, tb, u, xa, xb, un, sem, out_sem):
    q, yy = place[0], place[1]
    copies = []
    for b in range(4):
        at = pl.ds(b * SHARE, SHARE)
        copies.append(
            (
                pltpu.make_async_copy(ta.at[at, :], xa.at[b], sem.at[2 * b]),
                pltpu.make_async_copy(tb.at[at, :], xb.at[b], sem.at[2 * b + 1]),
            )
        )
    for c in copies:
        for t in c:
            t.start()
    ma, ra, mb, rb, _ = moments(sums, q)
    ns = []
    for p, m, s in ((pa, ma, ra), (pb, mb, rb)):
        n = (p[...] - m) * s
        rounded = n.astype(bf16)
        excess = jnp.sum(n - rounded.astype(f32), axis=0, keepdims=True)
        excess = jnp.concatenate([excess, jnp.zeros((15, BLOCK), f32)], axis=0).astype(bf16)
        ns.append(jnp.concatenate([rounded, excess, jnp.zeros((112, BLOCK), bf16)], axis=0))
    scale = U_SCALE / TOTAL
    done = []
    for b in range(4):
        for t in copies[b]:
            t.wait()
        un[b, :, :BLOCK] = dot(xb[b], ns[0], 1, 0) * scale
        un[b, :, BLOCK:] = dot(xa[b], ns[1], 1, 0) * scale
        out = pltpu.make_async_copy(un.at[b], u.at[b ^ yy], out_sem.at[b])
        out.start()
        done.append(out)
    for t in done:
        t.wait()


def combine(place, sums, pa, pb, *refs):
    ys, us, (out_a, out_b, ya, yb) = refs[:8], refs[8:16], refs[16:]
    q, yy = place[0], place[1]
    for j in range(4):
        for i in range(4):
            at = pl.multiple_of((q ^ j) * QUARTER + (i & 1) * 48, 16)
            for h in range(2):
                to = ya if i < 2 else yb
                to[pl.ds(at, 48), h * 768 : (h + 1) * 768] = ys[2 * j + i // 2][2 * (i & 1) + h]
    ma, ra, mb, rb, corr = moments(sums, q)
    for first, y, p, m, r, out in (
        (0, yb, pb, mb, rb, out_a),
        (BLOCK, ya, pa, ma, ra, out_b),
    ):
        acc = (p[...] - m) * (r * (corr - 2.0))
        cols = slice(first, first + BLOCK)
        for s in range(4):
            at = pl.ds(pl.multiple_of((yy ^ s) * SHARE, 128), SHARE)
            part = y[:, at]
            acc = acc + (dot(part, us[2 * s][:, cols], 1, 0) + dot(part, us[2 * s + 1][:, cols], 1, 0))
        out[...] = acc


def mark(arrived, out):
    out[...] = jnp.zeros(out.shape, f32)


def arrival(t, us):
    return pl.pallas_call(
        mark,
        out_shape=jax.ShapeDtypeStruct((8, 128), f32),
        in_specs=[ANY],
        out_specs=VMEM,
        cost_estimate=pl.CostEstimate(flops=us * 10**9, bytes_accessed=0, transcendentals=0),
        name="mark",
    )(t)


def hand_on(whole, ready, out):
    pass


def local(va, vb, w):
    q = lax.axis_index("xl") * 2 + lax.axis_index("c")
    place = jnp.stack([q, lax.axis_index("y")]).astype(jnp.int32)
    shape = jax.ShapeDtypeStruct
    sems = pltpu.SemaphoreType.DMA
    half = EARLY

    def swap(t, axis):
        return lax.ppermute(t, axis, SWAP)

    def along_y(t, s):
        return lax.ppermute(t, "y", [(i, i ^ s) for i in range(4)])

    w_c = swap(w, "c")
    w_x = swap(w[:half], "xl")

    pa, pb, own = call(
        project,
        (shape((ROWS, BLOCK), f32), shape((ROWS, BLOCK), f32), shape((32, 8, BLOCK), f32)),
        [ANY] * 3,
        4 * ROWS * DEPTH * BLOCK,
        4 * 2**20,
        [
            pltpu.VMEM((3, ROWS, DEPTH // 3), bf16),
            pltpu.VMEM((3, ROWS, DEPTH // 3), bf16),
            pltpu.VMEM((3, DEPTH // 3, BLOCK), bf16),
            sems((9,)),
        ],
        name="project",
    )(va, vb, w)
    sums = exchange(own, ("xh", "y", "xl", "c"))
    va, vb, pa = lax.optimization_barrier((va, vb, pa))
    ta, tb, v_quarter = call(
        turn,
        (shape((DEPTH, 512), bf16),) * 2 + (shape((2 * QUARTER, DEPTH), bf16),),
        [SMEM] + [VMEM] * 2,
        10 * 2**20,
        6 * 2**20,
        name="turn",
    )(place, va, vb)
    sums, ta, tb, v_quarter, w_late, w_x = lax.optimization_barrier(
        (sums, ta, tb, v_quarter, w[half:], w_x)
    )
    w_xb = swap(w_late, "xl")
    w_xcb = swap(w_xb, "c")

    u_parts = call(
        correlate,
        shape((4, SHARE, 2 * BLOCK), f32),
        [SMEM] + [VMEM] * 3 + [ANY] * 2,
        4 * ROWS * DEPTH * BLOCK,
        6 * 2**20,
        [
            pltpu.VMEM((4, SHARE, 512), bf16),
            pltpu.VMEM((4, SHARE, 512), bf16),
            pltpu.VMEM((4, SHARE, 2 * BLOCK), f32),
            sems((8,)),
            sems((4,)),
        ],
        out_specs=ANY,
        name="correlate",
    )(place, sums, pa, pb, ta, tb)
    u_parts, w_x = lax.optimization_barrier((u_parts, w_x))
    w_xc = swap(w_x, "c")
    u = u_parts[0]
    for s in (1, 2, 3):
        u = u + along_y(u_parts[s].astype(f16), s).astype(f32)
    u_near = arrival(u[:8, :128], 7)
    u = u.astype(f16)
    u = u.astype(f32) + swap(u, "xh").astype(f32)
    u_far = arrival(u[:8, :128], 6)
    u = lax.optimization_barrier(u.astype(f16))
    split = []
    for t in [u] + [along_y(u, s) for s in (1, 2, 3)]:
        t = t.astype(f32) * (1.0 / U_SCALE)
        high = lax.reduce_precision(t, 8, 7)
        split += [high.astype(bf16), (t - high).astype(bf16)]

    y_part = call(
        embed,
        shape((8,) + PIECE, bf16),
        [SMEM] + [VMEM] * 8,
        16 * ROWS * DEPTH * BLOCK // 2,
        7 * 2**20,
        [pltpu.VMEM((QUARTER, 4 * BLOCK), bf16)] * 2,
        name="embed",
        vmem=20,
    )(place, sums, v_quarter, w, w_c, w_x, w_xb, w_xc, w_xcb)
    y_copies = call(
        add_copies,
        shape((8,) + PIECE, bf16),
        [ANY] * 2,
        10 * 2**20,
        2**20,
        [pltpu.VMEM((8,) + PIECE, bf16), pltpu.VMEM(PIECE, bf16), sems, sems((8,))],
        out_specs=ANY,
        name="add_copies",
        vmem=63,
    )(exchange(y_part, "z"), u_near)
    y0 = pl.pallas_call(
        hand_on,
        out_shape=shape((8,) + PIECE, bf16),
        in_specs=[ANY, ANY],
        out_specs=ANY,
        input_output_aliases={0: 0},
        compiler_params=pltpu.CompilerParams(vmem_limit_bytes=63 * 2**20),
        name="hand_on",
    )(exchange(y_copies, "z"), u_far)
    y0 = [y0[:4], y0[4:]]
    y2 = [swap(t, "xl") for t in y0]
    y1 = [swap(t, "c") for t in y0]
    y3 = [swap(t, "c") for t in y2]

    return call(
        combine,
        (shape((ROWS, BLOCK), f32),) * 2,
        [SMEM] + [VMEM] * 19,
        8 * ROWS * DEPTH * BLOCK,
        8 * 2**20,
        [pltpu.VMEM((ROWS, DEPTH), bf16)] * 2,
        name="combine",
        vmem=20,
    )(place, sums, pa, pb, *y0, *y1, *y2, *y3, *split)


def solution(mesh):
    fine = Mesh(np.asarray(mesh.devices).reshape(tuple(PARTS.values())), tuple(PARTS))
    return jax.shard_map(
        local,
        mesh=fine,
        in_specs=(P(DP, None), P(DP, None), P(None, FEAT)),
        out_specs=(P(DP, FEAT), P(DP, FEAT)),
        check_vma=False,
    )
```

```python
import jax
import jax.numpy as jnp
import numpy as np
from jax import lax
from jax.experimental import pallas as pl
from jax.experimental.pallas import tpu as pltpu
from jax.sharding import Mesh, PartitionSpec as P

DP = ("xh", "y")
FEAT = ("z", "xl", "c")
PARTS = {"xh": 2, "y": 4, "z": 8, "xl": 2, "c": 2}
SWAP = [(0, 1), (1, 0)]
U_SCALE = 1024.0
EPS = 1e-05
f32, bf16, f16 = jnp.float32, jnp.bfloat16, jnp.float16

ROWS = 384
TOTAL = 3072
DEPTH = 1536
BLOCK = 256
QUARTER = ROWS // 4
PIECE = (48, 768)
SHARE = DEPTH // 4
EARLY = 1024
VMEM = pl.BlockSpec(memory_space=pltpu.VMEM)
SMEM = pl.BlockSpec(memory_space=pltpu.SMEM)
ANY = pl.BlockSpec(memory_space=pl.ANY)


def exchange(blocks, axes):
    return lax.all_to_all(blocks, axes, split_axis=0, concat_axis=0, tiled=True)


def dot(a, b, ca, cb):
    return lax.dot_general(a, b, (((ca,), (cb,)), ((), ())), preferred_element_type=f32)


def call(body, out, ins, flops, nbytes, scratch=(), name=None, out_specs=None, vmem=60):
    return pl.pallas_call(
        body,
        out_shape=out,
        in_specs=ins,
        out_specs=out_specs or jax.tree.map(lambda _: VMEM, out),
        scratch_shapes=scratch,
        compiler_params=pltpu.CompilerParams(vmem_limit_bytes=vmem * 2**20),
        cost_estimate=pl.CostEstimate(flops=flops, bytes_accessed=nbytes, transcendentals=0),
        name=name,
    )


def project(va, vb, w, pa, pb, sums, xa, xb, xw, sem):
    third = DEPTH // 3
    copies = []
    for k in range(3):
        at = pl.ds(k * third, third)
        copies.append(
            [
                pltpu.make_async_copy(va.at[:, at], xa.at[k], sem.at[3 * k]),
                pltpu.make_async_copy(vb.at[:, at], xb.at[k], sem.at[3 * k + 1]),
                pltpu.make_async_copy(w.at[at, :], xw.at[k], sem.at[3 * k + 2]),
            ]
        )
    for c in copies:
        for t in c:
            t.start()
    a = b = 0.0
    for k in range(3):
        for t in copies[k]:
            t.wait()
        a = a + dot(xa[k], xw[k], 1, 0)
        b = b + dot(xb[k], xw[k], 1, 0)
    pa[...] = a
    pb[...] = b
    col = [jnp.sum(t, axis=0, keepdims=True) for t in (a, a * a, b, b * b, a * b)]
    own = jnp.concatenate(col + [jnp.zeros((3, BLOCK), f32)], axis=0)
    sums[...] = jnp.broadcast_to(own[None], sums.shape)


def moments(sums, q):
    t = sums[q]
    for d in range(1, 8):
        t = t + sums[4 * d + q]
    t = t * (1.0 / TOTAL)
    ma, mb = t[0:1], t[2:3]
    ra = lax.rsqrt(t[1:2] - ma * ma + EPS)
    rb = lax.rsqrt(t[3:4] - mb * mb + EPS)
    return ma, ra, mb, rb, (t[4:5] - ma * mb) * ra * rb


def embed(place, sums, v, w0, w1, w2, w2b, w3, w3b, y, na, nb):
    q = place[0]
    half = EARLY
    ws = ((w0,), (w1,), (w2, w2b), (w3, w3b))
    for j, wj in enumerate(ws):
        ma, ra, mb, rb, _ = moments(sums, q ^ j)
        if len(wj) == 1:
            p = dot(v[...], wj[0][...], 1, 0)
        else:
            p = dot(v[:, :half], wj[0][...], 1, 0) + dot(v[:, half:], wj[1][...], 1, 0)
        cols = slice(j * BLOCK, (j + 1) * BLOCK)
        na[:, cols] = ((p[:QUARTER] - ma) * (ra * ra)).astype(bf16)
        nb[:, cols] = ((p[QUARTER:] - mb) * (rb * rb)).astype(bf16)
    n = jnp.concatenate([na[...], nb[...]], axis=0)
    for k in range(6):
        acc = 0.0
        for j, wj in enumerate(ws):
            late = len(wj) == 2 and k * 256 >= EARLY
            part = wj[1] if late else wj[0]
            first = k * 256 - (EARLY if late else 0)
            nj = n[:, j * BLOCK : (j + 1) * BLOCK]
            acc = acc + dot(nj, part[first : first + 256, :], 1, 1)
        acc = acc.astype(bf16)
        for i in range(4):
            y[2 * i + k // 3, :, (k % 3) * 256 : (k % 3 + 1) * 256] = acc[48 * i : 48 * i + 48]


def add_copies(parts, ready, out):
    total = parts[0].astype(f32)
    for d in range(1, 8):
        total = total + parts[d].astype(f32)
    out[...] = jnp.broadcast_to(total.astype(bf16)[None], out.shape)


def turn(place, va, vb, ta, tb, quarter):
    at = pl.ds(pl.multiple_of(place[0] * QUARTER, 32), QUARTER)
    quarter[:QUARTER] = va[at, :]
    quarter[QUARTER:] = vb[at, :]
    for view, out in ((va, ta), (vb, tb)):
        v = view[...]
        centre = jnp.sum(v.astype(f32), axis=0, keepdims=True) * (1.0 / ROWS)
        centre = jnp.concatenate([centre, jnp.zeros((15, DEPTH), f32)], axis=0).astype(bf16)
        out[...] = jnp.concatenate([v, centre, jnp.zeros((112, DEPTH), bf16)], axis=0).T


def correlate(place, sums, pa, pb, ta, tb, u0, u1, u2, u3, xs, xpa, xpb, xa, xb, un, sem, out_sem):
    q, yy = place[0], place[1]
    stats = [
        pltpu.make_async_copy(src, dst, sem.at[8 + i])
        for i, (src, dst) in enumerate(((sums, xs), (pa, xpa), (pb, xpb)))
    ]
    copies = {}
    for s in (1, 2, 3, 0):
        at = pl.ds(pl.multiple_of((s ^ yy) * SHARE, SHARE), SHARE)
        copies[s] = (
            pltpu.make_async_copy(ta.at[at, :], xa.at[s], sem.at[2 * s]),
            pltpu.make_async_copy(tb.at[at, :], xb.at[s], sem.at[2 * s + 1]),
        )
    for t in stats:
        t.start()
    for c in copies.values():
        for t in c:
            t.start()
    for t in stats:
        t.wait()
    ma, ra, mb, rb, _ = moments(xs, q)
    ns = []
    for p, m, s in ((xpa, ma, ra), (xpb, mb, rb)):
        n = (p[...] - m) * s
        rounded = n.astype(bf16)
        excess = jnp.sum(n - rounded.astype(f32), axis=0, keepdims=True)
        excess = jnp.concatenate([excess, jnp.zeros((15, BLOCK), f32)], axis=0).astype(bf16)
        ns.append(jnp.concatenate([rounded, excess, jnp.zeros((112, BLOCK), bf16)], axis=0))
    scale = U_SCALE / TOTAL
    done = []
    for s, u in ((1, u1), (2, u2), (3, u3), (0, u0)):
        for t in copies[s]:
            t.wait()
        un[s, :, :BLOCK] = dot(xb[s], ns[0], 1, 0) * scale
        un[s, :, BLOCK:] = dot(xa[s], ns[1], 1, 0) * scale
        out = pltpu.make_async_copy(un.at[s], u, out_sem.at[s])
        out.start()
        done.append(out)
    for t in done:
        t.wait()


def combine(place, sums, pa, pb, *refs):
    ys, us, (out_a, out_b, ya, yb) = refs[:8], refs[8:16], refs[16:]
    q, yy = place[0], place[1]
    for j in range(4):
        for i in range(4):
            at = pl.multiple_of((q ^ j) * QUARTER + (i & 1) * 48, 16)
            for h in range(2):
                to = ya if i < 2 else yb
                to[pl.ds(at, 48), h * 768 : (h + 1) * 768] = ys[2 * j + i // 2][2 * (i & 1) + h]
    ma, ra, mb, rb, corr = moments(sums, q)
    for first, y, p, m, r, out in (
        (0, yb, pb, mb, rb, out_a),
        (BLOCK, ya, pa, ma, ra, out_b),
    ):
        acc = (p[...] - m) * (r * (corr - 2.0))
        cols = slice(first, first + BLOCK)
        for s in range(4):
            at = pl.ds(pl.multiple_of((yy ^ s) * SHARE, 128), SHARE)
            part = y[:, at]
            acc = acc + (dot(part, us[2 * s][:, cols], 1, 0) + dot(part, us[2 * s + 1][:, cols], 1, 0))
        out[...] = acc


def mark(arrived, out):
    out[...] = jnp.zeros(out.shape, f32)


def arrival(t, us):
    return pl.pallas_call(
        mark,
        out_shape=jax.ShapeDtypeStruct((8, 128), f32),
        in_specs=[ANY],
        out_specs=VMEM,
        cost_estimate=pl.CostEstimate(flops=us * 10**9, bytes_accessed=0, transcendentals=0),
        name="mark",
    )(t)


def halve(whole, ready, first, second):
    first[...] = whole[:4]
    second[...] = whole[4:]


def local(va, vb, w):
    q = lax.axis_index("xl") * 2 + lax.axis_index("c")
    place = jnp.stack([q, lax.axis_index("y")]).astype(jnp.int32)
    shape = jax.ShapeDtypeStruct
    sems = pltpu.SemaphoreType.DMA
    half = EARLY

    def swap(t, axis):
        return lax.ppermute(t, axis, SWAP)

    def along_y(t, s):
        return lax.ppermute(t, "y", [(i, i ^ s) for i in range(4)])

    w_c = swap(w, "c")
    w_x = swap(w[:half], "xl")

    pa, pb, own = call(
        project,
        (shape((ROWS, BLOCK), f32), shape((ROWS, BLOCK), f32), shape((32, 8, BLOCK), f32)),
        [ANY] * 3,
        4 * ROWS * DEPTH * BLOCK,
        4 * 2**20,
        [
            pltpu.VMEM((3, ROWS, DEPTH // 3), bf16),
            pltpu.VMEM((3, ROWS, DEPTH // 3), bf16),
            pltpu.VMEM((3, DEPTH // 3, BLOCK), bf16),
            sems((9,)),
        ],
        name="project",
    )(va, vb, w)
    sums = exchange(own, ("xh", "y", "xl", "c"))
    va, vb, pa = lax.optimization_barrier((va, vb, pa))
    ta, tb, v_quarter = call(
        turn,
        (shape((DEPTH, 512), bf16),) * 2 + (shape((2 * QUARTER, DEPTH), bf16),),
        [SMEM] + [VMEM] * 2,
        10 * 2**20,
        6 * 2**20,
        name="turn",
    )(place, va, vb)
    sums, ta, tb, v_quarter, w_late, w_x = lax.optimization_barrier(
        (sums, ta, tb, v_quarter, w[half:], w_x)
    )
    w_xb = swap(w_late, "xl")
    w_xcb = swap(w_xb, "c")

    u_parts = call(
        correlate,
        (shape((SHARE, 2 * BLOCK), f32),) * 4,
        [SMEM] + [ANY] * 5,
        4 * ROWS * DEPTH * BLOCK,
        6 * 2**20,
        [
            pltpu.VMEM((32, 8, BLOCK), f32),
            pltpu.VMEM((ROWS, BLOCK), f32),
            pltpu.VMEM((ROWS, BLOCK), f32),
            pltpu.VMEM((4, SHARE, 512), bf16),
            pltpu.VMEM((4, SHARE, 512), bf16),
            pltpu.VMEM((4, SHARE, 2 * BLOCK), f32),
            sems((11,)),
            sems((4,)),
        ],
        out_specs=(ANY,) * 4,
        name="correlate",
    )(place, sums, pa, pb, ta, tb)
    *u_parts, w_x = lax.optimization_barrier((*u_parts, w_x))
    w_xc = swap(w_x, "c")
    u = u_parts[0]
    for s in (1, 2, 3):
        u = u + along_y(u_parts[s].astype(f16), s).astype(f32)
    u_near = arrival(u[:8, :128], 8)
    u = u.astype(f16)
    u = u.astype(f32) + swap(u, "xh").astype(f32)
    u_far = arrival(u[:8, :128], 4)
    u = lax.optimization_barrier(u.astype(f16))
    split = []
    for t in [u] + [along_y(u, s) for s in (1, 2, 3)]:
        t = t.astype(f32) * (1.0 / U_SCALE)
        high = lax.reduce_precision(t, 8, 7)
        split += [high.astype(bf16), (t - high).astype(bf16)]

    y_part = call(
        embed,
        shape((8,) + PIECE, bf16),
        [SMEM] + [VMEM] * 8,
        16 * ROWS * DEPTH * BLOCK // 2,
        7 * 2**20,
        [pltpu.VMEM((QUARTER, 4 * BLOCK), bf16)] * 2,
        name="embed",
        vmem=20,
    )(place, sums, v_quarter, w, w_c, w_x, w_xb, w_xc, w_xcb)
    y_copies = call(
        add_copies,
        shape((8,) + PIECE, bf16),
        [VMEM] * 2,
        10 * 2**20,
        2**20,
        name="add_copies",
        vmem=4,
    )(exchange(y_part, "z"), u_near)
    y0 = call(
        halve,
        (shape((4,) + PIECE, bf16),) * 2,
        [VMEM] * 2,
        0,
        2**20,
        name="halve",
        vmem=4,
    )(exchange(y_copies, "z"), u_far)
    y2 = [swap(t, "xl") for t in y0]
    y1 = [swap(t, "c") for t in y0]
    y2[1], *split = lax.optimization_barrier((y2[1], *split))
    y3 = [swap(t, "c") for t in y2]

    return call(
        combine,
        (shape((ROWS, BLOCK), f32),) * 2,
        [SMEM] + [VMEM] * 19,
        8 * ROWS * DEPTH * BLOCK,
        8 * 2**20,
        [pltpu.VMEM((ROWS, DEPTH), bf16)] * 2,
        name="combine",
        vmem=20,
    )(place, sums, pa, pb, *y0, *y1, *y2, *y3, *split)


def solution(mesh):
    fine = Mesh(np.asarray(mesh.devices).reshape(tuple(PARTS.values())), tuple(PARTS))
    return jax.shard_map(
        local,
        mesh=fine,
        in_specs=(P(DP, None), P(DP, None), P(None, FEAT)),
        out_specs=(P(DP, FEAT), P(DP, FEAT)),
        check_vma=False,
    )
```

```python
import jax
import jax.numpy as jnp
import numpy as np
from jax import lax
from jax.experimental import pallas as pl
from jax.experimental.pallas import tpu as pltpu
from jax.sharding import Mesh, PartitionSpec as P

DP = ("xh", "y")
FEAT = ("z", "xl", "c")
PARTS = {"xh": 2, "y": 4, "z": 8, "xl": 2, "c": 2}
SWAP = [(0, 1), (1, 0)]
U_SCALE = 1024.0
EPS = 1e-05
f32, bf16, f16 = jnp.float32, jnp.bfloat16, jnp.float16

ROWS = 384
TOTAL = 3072
DEPTH = 1536
BLOCK = 256
QUARTER = ROWS // 4
PIECE = (48, 768)
SHARE = DEPTH // 4
EARLY = 1024
VMEM = pl.BlockSpec(memory_space=pltpu.VMEM)
SMEM = pl.BlockSpec(memory_space=pltpu.SMEM)
ANY = pl.BlockSpec(memory_space=pl.ANY)


def exchange(blocks, axes):
    return lax.all_to_all(blocks, axes, split_axis=0, concat_axis=0, tiled=True)


def dot(a, b, ca, cb):
    return lax.dot_general(a, b, (((ca,), (cb,)), ((), ())), preferred_element_type=f32)


def call(body, out, ins, flops, nbytes, scratch=(), name=None, out_specs=None, vmem=60):
    return pl.pallas_call(
        body,
        out_shape=out,
        in_specs=ins,
        out_specs=out_specs or jax.tree.map(lambda _: VMEM, out),
        scratch_shapes=scratch,
        compiler_params=pltpu.CompilerParams(vmem_limit_bytes=vmem * 2**20),
        cost_estimate=pl.CostEstimate(flops=flops, bytes_accessed=nbytes, transcendentals=0),
        name=name,
    )


def project(va, vb, w, pa, pb, sums, xa, xb, xw, sem):
    third = DEPTH // 3
    copies = []
    for k in range(3):
        at = pl.ds(k * third, third)
        copies.append(
            [
                pltpu.make_async_copy(va.at[:, at], xa.at[k], sem.at[3 * k]),
                pltpu.make_async_copy(vb.at[:, at], xb.at[k], sem.at[3 * k + 1]),
                pltpu.make_async_copy(w.at[at, :], xw.at[k], sem.at[3 * k + 2]),
            ]
        )
    for c in copies:
        for t in c:
            t.start()
    a = b = 0.0
    for k in range(3):
        for t in copies[k]:
            t.wait()
        a = a + dot(xa[k], xw[k], 1, 0)
        b = b + dot(xb[k], xw[k], 1, 0)
    pa[...] = a
    pb[...] = b
    col = [jnp.sum(t, axis=0, keepdims=True) for t in (a, a * a, b, b * b, a * b)]
    own = jnp.concatenate(col + [jnp.zeros((3, BLOCK), f32)], axis=0)
    sums[...] = jnp.broadcast_to(own[None], sums.shape)


def moments(sums, q):
    t = sums[q]
    for d in range(1, 8):
        t = t + sums[4 * d + q]
    t = t * (1.0 / TOTAL)
    ma, mb = t[0:1], t[2:3]
    ra = lax.rsqrt(t[1:2] - ma * ma + EPS)
    rb = lax.rsqrt(t[3:4] - mb * mb + EPS)
    return ma, ra, mb, rb, (t[4:5] - ma * mb) * ra * rb


def embed(place, sums, v, w0, w1, w2, w2b, w3, w3b, y, na, nb):
    q = place[0]
    half = EARLY
    ws = ((w0,), (w1,), (w2, w2b), (w3, w3b))
    for j, wj in enumerate(ws):
        ma, ra, mb, rb, _ = moments(sums, q ^ j)
        if len(wj) == 1:
            p = dot(v[...], wj[0][...], 1, 0)
        else:
            p = dot(v[:, :half], wj[0][...], 1, 0) + dot(v[:, half:], wj[1][...], 1, 0)
        cols = slice(j * BLOCK, (j + 1) * BLOCK)
        na[:, cols] = ((p[:QUARTER] - ma) * (ra * ra)).astype(bf16)
        nb[:, cols] = ((p[QUARTER:] - mb) * (rb * rb)).astype(bf16)
    n = jnp.concatenate([na[...], nb[...]], axis=0)
    for k in range(6):
        acc = 0.0
        for j, wj in enumerate(ws):
            late = len(wj) == 2 and k * 256 >= EARLY
            part = wj[1] if late else wj[0]
            first = k * 256 - (EARLY if late else 0)
            nj = n[:, j * BLOCK : (j + 1) * BLOCK]
            acc = acc + dot(nj, part[first : first + 256, :], 1, 1)
        acc = acc.astype(bf16)
        for i in range(4):
            y[2 * i + k // 3, :, (k % 3) * 256 : (k % 3 + 1) * 256] = acc[48 * i : 48 * i + 48]


def add_copies(parts, ready, out):
    total = parts[0].astype(f32)
    for d in range(1, 8):
        total = total + parts[d].astype(f32)
    out[...] = jnp.broadcast_to(total.astype(bf16)[None], out.shape)


def turn(place, va, vb, ta, tb, quarter):
    at = pl.ds(pl.multiple_of(place[0] * QUARTER, 32), QUARTER)
    quarter[:QUARTER] = va[at, :]
    quarter[QUARTER:] = vb[at, :]
    for view, out in ((va, ta), (vb, tb)):
        v = view[...]
        centre = jnp.sum(v.astype(f32), axis=0, keepdims=True) * (1.0 / ROWS)
        centre = jnp.concatenate([centre, jnp.zeros((15, DEPTH), f32)], axis=0).astype(bf16)
        out[...] = jnp.concatenate([v, centre, jnp.zeros((112, DEPTH), bf16)], axis=0).T


def correlate(place, sums, pa, pb, ta, tb, u0, u1, u2, u3, xs, xpa, xpb, xa, xb, sem):
    q, yy = place[0], place[1]
    stats = [
        pltpu.make_async_copy(src, dst, sem.at[8 + i])
        for i, (src, dst) in enumerate(((sums, xs), (pa, xpa), (pb, xpb)))
    ]
    copies = {}
    for s in (1, 2, 3, 0):
        at = pl.ds(pl.multiple_of(((yy + s) & 3) * SHARE, SHARE), SHARE)
        copies[s] = (
            pltpu.make_async_copy(ta.at[at, :], xa.at[s], sem.at[2 * s]),
            pltpu.make_async_copy(tb.at[at, :], xb.at[s], sem.at[2 * s + 1]),
        )
    for t in stats:
        t.start()
    for c in copies.values():
        for t in c:
            t.start()
    for t in stats:
        t.wait()
    ma, ra, mb, rb, _ = moments(xs, q)
    ns = []
    for p, m, s in ((xpa, ma, ra), (xpb, mb, rb)):
        n = (p[...] - m) * s
        rounded = n.astype(bf16)
        excess = jnp.sum(n - rounded.astype(f32), axis=0, keepdims=True)
        excess = jnp.concatenate([excess, jnp.zeros((15, BLOCK), f32)], axis=0).astype(bf16)
        ns.append(jnp.concatenate([rounded, excess, jnp.zeros((112, BLOCK), bf16)], axis=0))
    scale = U_SCALE / TOTAL
    for s, u in ((1, u1), (2, u2), (3, u3), (0, u0)):
        for t in copies[s]:
            t.wait()
        u[:, :BLOCK] = dot(xb[s], ns[0], 1, 0) * scale
        u[:, BLOCK:] = dot(xa[s], ns[1], 1, 0) * scale


def combine(place, sums, pa, pb, *refs):
    ys, us, (out_a, out_b, ya, yb) = refs[:8], refs[8:16], refs[16:]
    q, yy = place[0], place[1]
    for j in range(4):
        for i in range(4):
            at = pl.multiple_of((q ^ j) * QUARTER + (i & 1) * 48, 16)
            for h in range(2):
                to = ya if i < 2 else yb
                to[pl.ds(at, 48), h * 768 : (h + 1) * 768] = ys[2 * j + i // 2][2 * (i & 1) + h]
    ma, ra, mb, rb, corr = moments(sums, q)
    for first, y, p, m, r, out in (
        (0, yb, pb, mb, rb, out_a),
        (BLOCK, ya, pa, ma, ra, out_b),
    ):
        acc = (p[...] - m) * (r * (corr - 2.0))
        cols = slice(first, first + BLOCK)
        for s in range(4):
            at = pl.ds(pl.multiple_of(((yy + 4 - s) & 3) * SHARE, 128), SHARE)
            part = y[:, at]
            acc = acc + (dot(part, us[2 * s][:, cols], 1, 0) + dot(part, us[2 * s + 1][:, cols], 1, 0))
        out[...] = acc


def mark(arrived, out):
    out[...] = jnp.zeros(out.shape, f32)


def arrival(t, us):
    return pl.pallas_call(
        mark,
        out_shape=jax.ShapeDtypeStruct((8, 128), f32),
        in_specs=[ANY],
        out_specs=VMEM,
        cost_estimate=pl.CostEstimate(flops=us * 10**9, bytes_accessed=0, transcendentals=0),
        name="mark",
    )(t)


def halve(whole, ready, first, second):
    first[...] = whole[:4]
    second[...] = whole[4:]


def local(va, vb, w):
    q = lax.axis_index("xl") * 2 + lax.axis_index("c")
    place = jnp.stack([q, lax.axis_index("y")]).astype(jnp.int32)
    shape = jax.ShapeDtypeStruct
    sems = pltpu.SemaphoreType.DMA
    half = EARLY

    def swap(t, axis):
        return lax.ppermute(t, axis, SWAP)

    def along_y(t, s):
        return lax.ppermute(t, "y", [(i, (i + s) % 4) for i in range(4)])

    w_c = swap(w, "c")
    w_x = swap(w[:half], "xl")

    pa, pb, own = call(
        project,
        (shape((ROWS, BLOCK), f32), shape((ROWS, BLOCK), f32), shape((32, 8, BLOCK), f32)),
        [ANY] * 3,
        4 * ROWS * DEPTH * BLOCK,
        4 * 2**20,
        [
            pltpu.VMEM((3, ROWS, DEPTH // 3), bf16),
            pltpu.VMEM((3, ROWS, DEPTH // 3), bf16),
            pltpu.VMEM((3, DEPTH // 3, BLOCK), bf16),
            sems((9,)),
        ],
        name="project",
    )(va, vb, w)
    sums = exchange(own, ("xh", "y", "xl", "c"))
    va, vb, pa = lax.optimization_barrier((va, vb, pa))
    ta, tb, v_quarter = call(
        turn,
        (shape((DEPTH, 512), bf16),) * 2 + (shape((2 * QUARTER, DEPTH), bf16),),
        [SMEM] + [VMEM] * 2,
        10 * 2**20,
        6 * 2**20,
        name="turn",
    )(place, va, vb)
    sums, ta, tb, v_quarter, w_late, w_x = lax.optimization_barrier(
        (sums, ta, tb, v_quarter, w[half:], w_x)
    )
    w_xb = swap(w_late, "xl")
    w_xcb = swap(w_xb, "c")

    u_parts = call(
        correlate,
        (shape((SHARE, 2 * BLOCK), f32),) * 4,
        [SMEM] + [ANY] * 5,
        4 * ROWS * DEPTH * BLOCK,
        6 * 2**20,
        [
            pltpu.VMEM((32, 8, BLOCK), f32),
            pltpu.VMEM((ROWS, BLOCK), f32),
            pltpu.VMEM((ROWS, BLOCK), f32),
            pltpu.VMEM((4, SHARE, 512), bf16),
            pltpu.VMEM((4, SHARE, 512), bf16),
            sems((11,)),
        ],
        name="correlate",
        vmem=20,
    )(place, sums, pa, pb, ta, tb)
    *u_parts, w_x = lax.optimization_barrier((*u_parts, w_x))
    w_xc = swap(w_x, "c")
    u = u_parts[0]
    for s in (1, 2, 3):
        u = u + along_y(u_parts[s].astype(f16), s).astype(f32)
    u_near = arrival(u[:8, :128], 8)
    u = u.astype(f16)
    u = u.astype(f32) + swap(u, "xh").astype(f32)
    u_far = arrival(u[:8, :128], 4)
    u = lax.optimization_barrier(u.astype(f16))
    us = [u] + [along_y(u, s) for s in (1, 2, 3)]

    y_part = call(
        embed,
        shape((8,) + PIECE, bf16),
        [SMEM] + [VMEM] * 8,
        16 * ROWS * DEPTH * BLOCK // 2,
        7 * 2**20,
        [pltpu.VMEM((QUARTER, 4 * BLOCK), bf16)] * 2,
        name="embed",
        vmem=20,
    )(place, sums, v_quarter, w, w_c, w_x, w_xb, w_xc, w_xcb)
    y_copies = call(
        add_copies,
        shape((8,) + PIECE, bf16),
        [VMEM] * 2,
        10 * 2**20,
        2**20,
        name="add_copies",
        vmem=4,
    )(exchange(y_part, "z"), u_near)
    y0 = call(
        halve,
        (shape((4,) + PIECE, bf16),) * 2,
        [VMEM] * 2,
        0,
        2**20,
        name="halve",
        vmem=4,
    )(exchange(y_copies, "z"), u_far)
    y2 = [swap(t, "xl") for t in y0]
    *y0, us[1], us[2], us[3] = lax.optimization_barrier((*y0, *us[1:]))
    split = []
    for t in us:
        t = t.astype(f32) * (1.0 / U_SCALE)
        high = lax.reduce_precision(t, 8, 7)
        split += [high.astype(bf16), (t - high).astype(bf16)]
    y1 = [swap(t, "c") for t in y0]
    y3 = [swap(t, "c") for t in y2]

    return call(
        combine,
        (shape((ROWS, BLOCK), f32),) * 2,
        [SMEM] + [VMEM] * 19,
        8 * ROWS * DEPTH * BLOCK,
        8 * 2**20,
        [pltpu.VMEM((ROWS, DEPTH), bf16)] * 2,
        name="combine",
        vmem=20,
    )(place, sums, pa, pb, *y0, *y1, *y2, *y3, *split)


def solution(mesh):
    fine = Mesh(np.asarray(mesh.devices).reshape(tuple(PARTS.values())), tuple(PARTS))
    return jax.shard_map(
        local,
        mesh=fine,
        in_specs=(P(DP, None), P(DP, None), P(None, FEAT)),
        out_specs=(P(DP, FEAT), P(DP, FEAT)),
        check_vma=False,
    )
```

```python
import jax
import jax.numpy as jnp
import numpy as np
from jax import lax
from jax.experimental import pallas as pl
from jax.experimental.pallas import tpu as pltpu
from jax.sharding import Mesh, PartitionSpec as P

DP = ("xh", "y")
FEAT = ("z", "xl", "c")
PARTS = {"xh": 2, "y": 4, "z": 8, "xl": 2, "c": 2}
SWAP = [(0, 1), (1, 0)]
U_SCALE = 1024.0
EPS = 1e-05
f32, bf16, f16 = jnp.float32, jnp.bfloat16, jnp.float16

ROWS = 384
TOTAL = 3072
DEPTH = 1536
BLOCK = 256
QUARTER = ROWS // 4
PIECE = (48, 768)
SHARE = DEPTH // 4
EARLY = 1024
VMEM = pl.BlockSpec(memory_space=pltpu.VMEM)
SMEM = pl.BlockSpec(memory_space=pltpu.SMEM)
ANY = pl.BlockSpec(memory_space=pl.ANY)


def exchange(blocks, axes):
    return lax.all_to_all(blocks, axes, split_axis=0, concat_axis=0, tiled=True)


def dot(a, b, ca, cb):
    return lax.dot_general(a, b, (((ca,), (cb,)), ((), ())), preferred_element_type=f32)


def call(body, out, ins, flops, nbytes, scratch=(), name=None, out_specs=None, vmem=60):
    return pl.pallas_call(
        body,
        out_shape=out,
        in_specs=ins,
        out_specs=out_specs or jax.tree.map(lambda _: VMEM, out),
        scratch_shapes=scratch,
        compiler_params=pltpu.CompilerParams(vmem_limit_bytes=vmem * 2**20),
        cost_estimate=pl.CostEstimate(flops=flops, bytes_accessed=nbytes, transcendentals=0),
        name=name,
    )


def project(va, vb, w, pa, pb, sums, xa, xb, xw, sem):
    third = DEPTH // 3
    copies = []
    for k in range(3):
        at = pl.ds(k * third, third)
        copies.append(
            [
                pltpu.make_async_copy(va.at[:, at], xa.at[k], sem.at[3 * k]),
                pltpu.make_async_copy(vb.at[:, at], xb.at[k], sem.at[3 * k + 1]),
                pltpu.make_async_copy(w.at[at, :], xw.at[k], sem.at[3 * k + 2]),
            ]
        )
    for c in copies:
        for t in c:
            t.start()
    a = b = 0.0
    for k in range(3):
        for t in copies[k]:
            t.wait()
        a = a + dot(xa[k], xw[k], 1, 0)
        b = b + dot(xb[k], xw[k], 1, 0)
    pa[...] = a
    pb[...] = b
    col = [jnp.sum(t, axis=0, keepdims=True) for t in (a, a * a, b, b * b, a * b)]
    own = jnp.concatenate(col + [jnp.zeros((3, BLOCK), f32)], axis=0)
    sums[...] = jnp.broadcast_to(own[None], sums.shape)


def moments(sums, q):
    t = sums[q]
    for d in range(1, 8):
        t = t + sums[4 * d + q]
    t = t * (1.0 / TOTAL)
    ma, mb = t[0:1], t[2:3]
    ra = lax.rsqrt(t[1:2] - ma * ma + EPS)
    rb = lax.rsqrt(t[3:4] - mb * mb + EPS)
    return ma, ra, mb, rb, (t[4:5] - ma * mb) * ra * rb


def embed(place, sums, v, w0, w1, w2, w2b, w3, w3b, y, na, nb):
    q = place[0]
    half = EARLY
    ws = ((w0,), (w1,), (w2, w2b), (w3, w3b))
    for j, wj in enumerate(ws):
        ma, ra, mb, rb, _ = moments(sums, q ^ j)
        if len(wj) == 1:
            p = dot(v[...], wj[0][...], 1, 0)
        else:
            p = dot(v[:, :half], wj[0][...], 1, 0) + dot(v[:, half:], wj[1][...], 1, 0)
        cols = slice(j * BLOCK, (j + 1) * BLOCK)
        na[:, cols] = ((p[:QUARTER] - ma) * (ra * ra)).astype(bf16)
        nb[:, cols] = ((p[QUARTER:] - mb) * (rb * rb)).astype(bf16)
    n = jnp.concatenate([na[...], nb[...]], axis=0)
    for k in range(6):
        acc = 0.0
        for j, wj in enumerate(ws):
            late = len(wj) == 2 and k * 256 >= EARLY
            part = wj[1] if late else wj[0]
            first = k * 256 - (EARLY if late else 0)
            nj = n[:, j * BLOCK : (j + 1) * BLOCK]
            acc = acc + dot(nj, part[first : first + 256, :], 1, 1)
        acc = acc.astype(bf16)
        for i in range(4):
            y[2 * i + k // 3, :, (k % 3) * 256 : (k % 3 + 1) * 256] = acc[48 * i : 48 * i + 48]


def add_copies(parts, ready, out):
    total = parts[0].astype(f32)
    for d in range(1, 8):
        total = total + parts[d].astype(f32)
    out[...] = jnp.broadcast_to(total.astype(bf16)[None], out.shape)


def turn(place, va, vb, ta, tb, quarter):
    at = pl.ds(pl.multiple_of(place[0] * QUARTER, 32), QUARTER)
    quarter[:QUARTER] = va[at, :]
    quarter[QUARTER:] = vb[at, :]
    for view, out in ((va, ta), (vb, tb)):
        v = view[...]
        centre = jnp.sum(v.astype(f32), axis=0, keepdims=True) * (1.0 / ROWS)
        centre = jnp.concatenate([centre, jnp.zeros((15, DEPTH), f32)], axis=0).astype(bf16)
        out[...] = jnp.concatenate([v, centre, jnp.zeros((112, DEPTH), bf16)], axis=0).T


def correlate(place, sums, pa, pb, ta, tb, u0, u1, u2, u3, xs, xpa, xpb, xa, xb, x0, x1, x2, x3, sem, out_sem):
    q, yy = place[0], place[1]
    stats = [
        pltpu.make_async_copy(src, dst, sem.at[8 + i])
        for i, (src, dst) in enumerate(((sums, xs), (pa, xpa), (pb, xpb)))
    ]
    copies = {}
    for s in (1, 2, 3, 0):
        at = pl.ds(pl.multiple_of(((yy + s) & 3) * SHARE, SHARE), SHARE)
        copies[s] = (
            pltpu.make_async_copy(ta.at[at, :], xa.at[s], sem.at[2 * s]),
            pltpu.make_async_copy(tb.at[at, :], xb.at[s], sem.at[2 * s + 1]),
        )
    for t in stats:
        t.start()
    for c in copies.values():
        for t in c:
            t.start()
    for t in stats:
        t.wait()
    ma, ra, mb, rb, _ = moments(xs, q)
    ns = []
    for p, m, s in ((xpa, ma, ra), (xpb, mb, rb)):
        n = (p[...] - m) * s
        rounded = n.astype(bf16)
        excess = jnp.sum(n - rounded.astype(f32), axis=0, keepdims=True)
        excess = jnp.concatenate([excess, jnp.zeros((15, BLOCK), f32)], axis=0).astype(bf16)
        ns.append(jnp.concatenate([rounded, excess, jnp.zeros((112, BLOCK), bf16)], axis=0))
    scale = U_SCALE / TOTAL
    done = []
    for s, x, u in ((1, x1, u1), (2, x2, u2), (3, x3, u3), (0, x0, u0)):
        for t in copies[s]:
            t.wait()
        x[:, :BLOCK] = (dot(xb[s], ns[0], 1, 0) * scale).astype(x.dtype)
        x[:, BLOCK:] = (dot(xa[s], ns[1], 1, 0) * scale).astype(x.dtype)
        out = pltpu.make_async_copy(x, u, out_sem.at[s])
        out.start()
        done.append(out)
    for t in done:
        t.wait()


def combine(place, sums, pa, pb, *refs):
    ys, us, (out_a, out_b, ya, yb) = refs[:8], refs[8:16], refs[16:]
    q, yy = place[0], place[1]
    for j in range(4):
        for i in range(4):
            at = pl.multiple_of((q ^ j) * QUARTER + (i & 1) * 48, 16)
            for h in range(2):
                to = ya if i < 2 else yb
                to[pl.ds(at, 48), h * 768 : (h + 1) * 768] = ys[2 * j + i // 2][2 * (i & 1) + h]
    ma, ra, mb, rb, corr = moments(sums, q)
    for first, y, p, m, r, out in (
        (0, yb, pb, mb, rb, out_a),
        (BLOCK, ya, pa, ma, ra, out_b),
    ):
        acc = (p[...] - m) * (r * (corr - 2.0))
        cols = slice(first, first + BLOCK)
        for s in range(4):
            at = pl.ds(pl.multiple_of(((yy + 4 - s) & 3) * SHARE, 128), SHARE)
            part = y[:, at]
            acc = acc + (dot(part, us[2 * s][:, cols], 1, 0) + dot(part, us[2 * s + 1][:, cols], 1, 0))
        out[...] = acc


def mark(arrived, out):
    out[...] = jnp.zeros(out.shape, f32)


def arrival(t, us):
    return pl.pallas_call(
        mark,
        out_shape=jax.ShapeDtypeStruct((8, 128), f32),
        in_specs=[ANY],
        out_specs=VMEM,
        cost_estimate=pl.CostEstimate(flops=us * 10**9, bytes_accessed=0, transcendentals=0),
        name="mark",
    )(t)


def halve(whole, ready, first, second):
    first[...] = whole[:4]
    second[...] = whole[4:]


def local(va, vb, w):
    q = lax.axis_index("xl") * 2 + lax.axis_index("c")
    place = jnp.stack([q, lax.axis_index("y")]).astype(jnp.int32)
    shape = jax.ShapeDtypeStruct
    sems = pltpu.SemaphoreType.DMA
    half = EARLY

    def swap(t, axis):
        return lax.ppermute(t, axis, SWAP)

    def along_y(t, s):
        return lax.ppermute(t, "y", [(i, (i + s) % 4) for i in range(4)])

    w_c = swap(w, "c")
    w_x = swap(w[:half], "xl")

    pa, pb, own = call(
        project,
        (shape((ROWS, BLOCK), f32), shape((ROWS, BLOCK), f32), shape((32, 8, BLOCK), f32)),
        [ANY] * 3,
        4 * ROWS * DEPTH * BLOCK,
        4 * 2**20,
        [
            pltpu.VMEM((3, ROWS, DEPTH // 3), bf16),
            pltpu.VMEM((3, ROWS, DEPTH // 3), bf16),
            pltpu.VMEM((3, DEPTH // 3, BLOCK), bf16),
            sems((9,)),
        ],
        name="project",
    )(va, vb, w)
    sums = exchange(own, ("xh", "y", "xl", "c"))
    va, vb, pa = lax.optimization_barrier((va, vb, pa))
    ta, tb, v_quarter = call(
        turn,
        (shape((DEPTH, 512), bf16),) * 2 + (shape((2 * QUARTER, DEPTH), bf16),),
        [SMEM] + [VMEM] * 2,
        10 * 2**20,
        6 * 2**20,
        name="turn",
    )(place, va, vb)
    sums, ta, tb, v_quarter, w_late, w_x = lax.optimization_barrier(
        (sums, ta, tb, v_quarter, w[half:], w_x)
    )
    w_xb = swap(w_late, "xl")
    w_xcb = swap(w_xb, "c")

    u_parts = call(
        correlate,
        (shape((SHARE, 2 * BLOCK), f32),) + (shape((SHARE, 2 * BLOCK), bf16),) * 3,
        [SMEM] + [ANY] * 5,
        4 * ROWS * DEPTH * BLOCK,
        6 * 2**20,
        [
            pltpu.VMEM((32, 8, BLOCK), f32),
            pltpu.VMEM((ROWS, BLOCK), f32),
            pltpu.VMEM((ROWS, BLOCK), f32),
            pltpu.VMEM((4, SHARE, 512), bf16),
            pltpu.VMEM((4, SHARE, 512), bf16),
            pltpu.VMEM((SHARE, 2 * BLOCK), f32),
            pltpu.VMEM((SHARE, 2 * BLOCK), bf16),
            pltpu.VMEM((SHARE, 2 * BLOCK), bf16),
            pltpu.VMEM((SHARE, 2 * BLOCK), bf16),
            sems((11,)),
            sems((4,)),
        ],
        out_specs=(ANY,) * 4,
        name="correlate",
    )(place, sums, pa, pb, ta, tb)
    *u_parts, w_x = lax.optimization_barrier((*u_parts, w_x))
    w_xc = swap(w_x, "c")
    u = u_parts[0]
    for s in (1, 2, 3):
        u = u + along_y(u_parts[s], s).astype(f32)
    u_near = arrival(u[:8, :128], 8)
    u = u.astype(f16)
    u = u.astype(f32) + swap(u, "xh").astype(f32)
    u_far = arrival(u[:8, :128], 4)
    u = lax.optimization_barrier(u.astype(f16))
    us = [u] + [along_y(u, s) for s in (1, 2, 3)]

    y_part = call(
        embed,
        shape((8,) + PIECE, bf16),
        [SMEM] + [VMEM] * 8,
        16 * ROWS * DEPTH * BLOCK // 2,
        7 * 2**20,
        [pltpu.VMEM((QUARTER, 4 * BLOCK), bf16)] * 2,
        name="embed",
        vmem=20,
    )(place, sums, v_quarter, w, w_c, w_x, w_xb, w_xc, w_xcb)
    y_copies = call(
        add_copies,
        shape((8,) + PIECE, bf16),
        [VMEM] * 2,
        10 * 2**20,
        2**20,
        name="add_copies",
        vmem=4,
    )(exchange(y_part, "z"), u_near)
    y0 = call(
        halve,
        (shape((4,) + PIECE, bf16),) * 2,
        [VMEM] * 2,
        0,
        2**20,
        name="halve",
        vmem=4,
    )(exchange(y_copies, "z"), u_far)
    y2 = [swap(t, "xl") for t in y0]
    *y0, us[1], us[2], us[3] = lax.optimization_barrier((*y0, *us[1:]))
    split = []
    for t in us:
        t = t.astype(f32) * (1.0 / U_SCALE)
        high = lax.reduce_precision(t, 8, 7)
        split += [high.astype(bf16), (t - high).astype(bf16)]
    y1 = [swap(t, "c") for t in y0]
    y2[1], *split = lax.optimization_barrier((y2[1], *split))
    y3 = [swap(t, "c") for t in y2]

    return call(
        combine,
        (shape((ROWS, BLOCK), f32),) * 2,
        [SMEM] + [VMEM] * 19,
        8 * ROWS * DEPTH * BLOCK,
        8 * 2**20,
        [pltpu.VMEM((ROWS, DEPTH), bf16)] * 2,
        name="combine",
        vmem=20,
    )(place, sums, pa, pb, *y0, *y1, *y2, *y3, *split)


def solution(mesh):
    fine = Mesh(np.asarray(mesh.devices).reshape(tuple(PARTS.values())), tuple(PARTS))
    return jax.shard_map(
        local,
        mesh=fine,
        in_specs=(P(DP, None), P(DP, None), P(None, FEAT)),
        out_specs=(P(DP, FEAT), P(DP, FEAT)),
        check_vma=False,
    )
```

```python
import jax
import jax.numpy as jnp
import numpy as np
from jax import lax
from jax.experimental import pallas as pl
from jax.experimental.pallas import tpu as pltpu
from jax.sharding import Mesh, PartitionSpec as P

DP = ("xh", "y")
FEAT = ("z", "xl", "c")
PARTS = {"xh": 2, "y": 4, "z": 8, "xl": 2, "c": 2}
SWAP = [(0, 1), (1, 0)]
U_SCALE = 1024.0
EPS = 1e-05
f32, bf16, f16 = jnp.float32, jnp.bfloat16, jnp.float16

ROWS = 384
TOTAL = 3072
DEPTH = 1536
BLOCK = 256
QUARTER = ROWS // 4
PIECE = (48, 768)
NEAR, FAR = (0, 1, 7, 2), (6, 3, 5, 4)
SHARE = DEPTH // 4
EARLY = 1024
VMEM = pl.BlockSpec(memory_space=pltpu.VMEM)
SMEM = pl.BlockSpec(memory_space=pltpu.SMEM)
ANY = pl.BlockSpec(memory_space=pl.ANY)


def exchange(blocks, axes):
    return lax.all_to_all(blocks, axes, split_axis=0, concat_axis=0, tiled=True)


def dot(a, b, ca, cb):
    return lax.dot_general(a, b, (((ca,), (cb,)), ((), ())), preferred_element_type=f32)


def call(body, out, ins, flops, nbytes, scratch=(), name=None, out_specs=None, vmem=60):
    return pl.pallas_call(
        body,
        out_shape=out,
        in_specs=ins,
        out_specs=out_specs or jax.tree.map(lambda _: VMEM, out),
        scratch_shapes=scratch,
        compiler_params=pltpu.CompilerParams(vmem_limit_bytes=vmem * 2**20),
        cost_estimate=pl.CostEstimate(flops=flops, bytes_accessed=nbytes, transcendentals=0),
        name=name,
    )


def project(va, vb, w, pa, pb, sums, xa, xb, xw, sem):
    third = DEPTH // 3
    copies = []
    for k in range(3):
        at = pl.ds(k * third, third)
        copies.append(
            [
                pltpu.make_async_copy(va.at[:, at], xa.at[k], sem.at[3 * k]),
                pltpu.make_async_copy(vb.at[:, at], xb.at[k], sem.at[3 * k + 1]),
                pltpu.make_async_copy(w.at[at, :], xw.at[k], sem.at[3 * k + 2]),
            ]
        )
    for c in copies:
        for t in c:
            t.start()
    a = b = 0.0
    for k in range(3):
        for t in copies[k]:
            t.wait()
        a = a + dot(xa[k], xw[k], 1, 0)
        b = b + dot(xb[k], xw[k], 1, 0)
    pa[...] = a
    pb[...] = b
    col = [jnp.sum(t, axis=0, keepdims=True) for t in (a, a * a, b, b * b, a * b)]
    own = jnp.concatenate(col + [jnp.zeros((3, BLOCK), f32)], axis=0)
    sums[...] = jnp.broadcast_to(own[None], sums.shape)


def moments(sums, q):
    t = sums[q]
    for d in range(1, 8):
        t = t + sums[4 * d + q]
    t = t * (1.0 / TOTAL)
    ma, mb = t[0:1], t[2:3]
    ra = lax.rsqrt(t[1:2] - ma * ma + EPS)
    rb = lax.rsqrt(t[3:4] - mb * mb + EPS)
    return ma, ra, mb, rb, (t[4:5] - ma * mb) * ra * rb


def embed(place, sums, v, w0, w1, w2, w2b, w3, w3b, *refs):
    ys, (na, nb, y) = refs[:8], refs[8:]
    q, z = place[0], place[2]
    half = EARLY
    ws = ((w0,), (w1,), (w2, w2b), (w3, w3b))
    for j, wj in enumerate(ws):
        ma, ra, mb, rb, _ = moments(sums, q ^ j)
        if len(wj) == 1:
            p = dot(v[...], wj[0][...], 1, 0)
        else:
            p = dot(v[:, :half], wj[0][...], 1, 0) + dot(v[:, half:], wj[1][...], 1, 0)
        cols = slice(j * BLOCK, (j + 1) * BLOCK)
        na[:, cols] = ((p[:QUARTER] - ma) * (ra * ra)).astype(bf16)
        nb[:, cols] = ((p[QUARTER:] - mb) * (rb * rb)).astype(bf16)
    n = jnp.concatenate([na[...], nb[...]], axis=0)
    for k in range(6):
        acc = 0.0
        for j, wj in enumerate(ws):
            late = len(wj) == 2 and k * 256 >= EARLY
            part = wj[1] if late else wj[0]
            first = k * 256 - (EARLY if late else 0)
            nj = n[:, j * BLOCK : (j + 1) * BLOCK]
            acc = acc + dot(nj, part[first : first + 256, :], 1, 1)
        acc = acc.astype(bf16)
        for i in range(4):
            y[2 * i + k // 3, :, (k % 3) * 256 : (k % 3 + 1) * 256] = acc[48 * i : 48 * i + 48]
    for s in range(8):
        ys[s][...] = y[(z + s) & 7]


def add(ready, *refs):
    parts, out = refs[:8], refs[8]
    total = parts[0][...].astype(f32)
    for t in parts[1:]:
        total = total + t[...].astype(f32)
    out[...] = total.astype(bf16)


def join(p0, p1, p2, p3, *refs):
    out = refs[-1]
    for i, t in enumerate((p0, p1, p2, p3)):
        out[i] = t[...]


def turn(place, va, vb, ta, tb, quarter):
    at = pl.ds(pl.multiple_of(place[0] * QUARTER, 32), QUARTER)
    quarter[:QUARTER] = va[at, :]
    quarter[QUARTER:] = vb[at, :]
    for view, out in ((va, ta), (vb, tb)):
        v = view[...]
        centre = jnp.sum(v.astype(f32), axis=0, keepdims=True) * (1.0 / ROWS)
        centre = jnp.concatenate([centre, jnp.zeros((15, DEPTH), f32)], axis=0).astype(bf16)
        out[...] = jnp.concatenate([v, centre, jnp.zeros((112, DEPTH), bf16)], axis=0).T


def correlate(place, sums, pa, pb, ta, tb, u0, u1, u2, u3, xs, xpa, xpb, xa, xb, x0, x1, x2, x3, sem, out_sem):
    q, yy = place[0], place[1]
    stats = [
        pltpu.make_async_copy(src, dst, sem.at[8 + i])
        for i, (src, dst) in enumerate(((sums, xs), (pa, xpa), (pb, xpb)))
    ]
    copies = {}
    for s in (1, 2, 3, 0):
        at = pl.ds(pl.multiple_of(((yy + s) & 3) * SHARE, SHARE), SHARE)
        copies[s] = (
            pltpu.make_async_copy(ta.at[at, :], xa.at[s], sem.at[2 * s]),
            pltpu.make_async_copy(tb.at[at, :], xb.at[s], sem.at[2 * s + 1]),
        )
    for t in stats:
        t.start()
    for c in copies.values():
        for t in c:
            t.start()
    for t in stats:
        t.wait()
    ma, ra, mb, rb, _ = moments(xs, q)
    ns = []
    for p, m, s in ((xpa, ma, ra), (xpb, mb, rb)):
        n = (p[...] - m) * s
        rounded = n.astype(bf16)
        excess = jnp.sum(n - rounded.astype(f32), axis=0, keepdims=True)
        excess = jnp.concatenate([excess, jnp.zeros((15, BLOCK), f32)], axis=0).astype(bf16)
        ns.append(jnp.concatenate([rounded, excess, jnp.zeros((112, BLOCK), bf16)], axis=0))
    scale = U_SCALE / TOTAL
    done = []
    for s, x, u in ((1, x1, u1), (2, x2, u2), (3, x3, u3), (0, x0, u0)):
        for t in copies[s]:
            t.wait()
        x[:, :BLOCK] = (dot(xb[s], ns[0], 1, 0) * scale).astype(x.dtype)
        x[:, BLOCK:] = (dot(xa[s], ns[1], 1, 0) * scale).astype(x.dtype)
        out = pltpu.make_async_copy(x, u, out_sem.at[s])
        out.start()
        done.append(out)
    for t in done:
        t.wait()


def combine(place, sums, pa, pb, *refs):
    ys, us, (out_a, out_b, y) = refs[:8], refs[8:16], refs[16:]
    q, yy, z = place[0], place[1], place[2]
    for n, s in enumerate(NEAR + FAR):
        piece = (z + 8 - s) & 7
        cols = pl.ds(pl.multiple_of((piece & 1) * 768, 128), 768)
        for j in range(4):
            rows = pl.multiple_of((q ^ j) * QUARTER + ((piece >> 1) & 1) * 48, 16)
            y[piece >> 2, pl.ds(rows, 48), cols] = ys[2 * j + n // 4][n % 4]
    ma, ra, mb, rb, corr = moments(sums, q)
    for first, view, p, m, r, out in (
        (0, 1, pb, mb, rb, out_a),
        (BLOCK, 0, pa, ma, ra, out_b),
    ):
        acc = (p[...] - m) * (r * (corr - 2.0))
        cols = slice(first, first + BLOCK)
        for s in range(4):
            at = pl.ds(pl.multiple_of(((yy + 4 - s) & 3) * SHARE, 128), SHARE)
            part = y[view, :, at]
            acc = acc + (dot(part, us[2 * s][:, cols], 1, 0) + dot(part, us[2 * s + 1][:, cols], 1, 0))
        out[...] = acc


def mark(arrived, out):
    out[...] = jnp.zeros(out.shape, f32)


def arrival(t, us):
    return pl.pallas_call(
        mark,
        out_shape=jax.ShapeDtypeStruct((8, 128), f32),
        in_specs=[ANY],
        out_specs=VMEM,
        cost_estimate=pl.CostEstimate(flops=us * 10**9, bytes_accessed=0, transcendentals=0),
        name="mark",
    )(t)


def local(va, vb, w):
    q = lax.axis_index("xl") * 2 + lax.axis_index("c")
    place = jnp.stack([q, lax.axis_index("y"), lax.axis_index("z")]).astype(jnp.int32)
    shape = jax.ShapeDtypeStruct
    sems = pltpu.SemaphoreType.DMA
    half = EARLY

    def swap(t, axis):
        return lax.ppermute(t, axis, SWAP)

    def along_z(t, s):
        return lax.ppermute(t, "z", [(i, (i + s) % 8) for i in range(8)])

    def along_y(t, s):
        return lax.ppermute(t, "y", [(i, (i + s) % 4) for i in range(4)])

    w_c = swap(w, "c")
    w_x = swap(w[:half], "xl")

    pa, pb, own = call(
        project,
        (shape((ROWS, BLOCK), f32), shape((ROWS, BLOCK), f32), shape((32, 8, BLOCK), f32)),
        [ANY] * 3,
        4 * ROWS * DEPTH * BLOCK,
        4 * 2**20,
        [
            pltpu.VMEM((3, ROWS, DEPTH // 3), bf16),
            pltpu.VMEM((3, ROWS, DEPTH // 3), bf16),
            pltpu.VMEM((3, DEPTH // 3, BLOCK), bf16),
            sems((9,)),
        ],
        name="project",
    )(va, vb, w)
    sums = exchange(own, ("xh", "y", "xl", "c"))
    va, vb, pa = lax.optimization_barrier((va, vb, pa))
    ta, tb, v_quarter = call(
        turn,
        (shape((DEPTH, 512), bf16),) * 2 + (shape((2 * QUARTER, DEPTH), bf16),),
        [SMEM] + [VMEM] * 2,
        10 * 2**20,
        6 * 2**20,
        name="turn",
    )(place, va, vb)
    sums, ta, tb, v_quarter, w_late, w_x = lax.optimization_barrier(
        (sums, ta, tb, v_quarter, w[half:], w_x)
    )
    w_xb = swap(w_late, "xl")
    w_xcb = swap(w_xb, "c")

    u_parts = call(
        correlate,
        (shape((SHARE, 2 * BLOCK), f32),) + (shape((SHARE, 2 * BLOCK), bf16),) * 3,
        [SMEM] + [ANY] * 5,
        4 * ROWS * DEPTH * BLOCK,
        6 * 2**20,
        [
            pltpu.VMEM((32, 8, BLOCK), f32),
            pltpu.VMEM((ROWS, BLOCK), f32),
            pltpu.VMEM((ROWS, BLOCK), f32),
            pltpu.VMEM((4, SHARE, 512), bf16),
            pltpu.VMEM((4, SHARE, 512), bf16),
            pltpu.VMEM((SHARE, 2 * BLOCK), f32),
            pltpu.VMEM((SHARE, 2 * BLOCK), bf16),
            pltpu.VMEM((SHARE, 2 * BLOCK), bf16),
            pltpu.VMEM((SHARE, 2 * BLOCK), bf16),
            sems((11,)),
            sems((4,)),
        ],
        out_specs=(ANY,) * 4,
        name="correlate",
    )(place, sums, pa, pb, ta, tb)
    *u_parts, w_x = lax.optimization_barrier((*u_parts, w_x))
    w_xc = swap(w_x, "c")
    u = u_parts[0]
    for s in (1, 2, 3):
        u = u + along_y(u_parts[s], s).astype(f32)
    u_near = arrival(u[:8, :128], 8)
    u = u.astype(f16)
    u = u.astype(f32) + swap(u, "xh").astype(f32)
    u_far = arrival(u[:8, :128], 4)
    u = lax.optimization_barrier(u.astype(f16))
    us = [u] + [along_y(u, s) for s in (1, 2, 3)]

    y_parts = call(
        embed,
        (shape(PIECE, bf16),) * 8,
        [SMEM] + [VMEM] * 8,
        16 * ROWS * DEPTH * BLOCK // 2,
        7 * 2**20,
        [pltpu.VMEM((QUARTER, 4 * BLOCK), bf16)] * 2 + [pltpu.VMEM((8,) + PIECE, bf16)],
        name="embed",
        vmem=20,
    )(place, sums, v_quarter, w, w_c, w_x, w_xb, w_xc, w_xcb)
    y_own = call(
        add,
        shape(PIECE, bf16),
        [ANY] + [VMEM] * 8,
        10 * 2**20,
        2**20,
        name="add",
        vmem=4,
    )(u_near, *[along_z(y_parts[s], s) if s else y_parts[0] for s in NEAR + FAR])
    y0 = []
    for group in (NEAR, FAR):
        pieces = [along_z(y_own, s) if s else y_own for s in group]
        ready = [u_far] if group == FAR else []
        y0.append(
            call(
                join,
                shape((4,) + PIECE, bf16),
                [VMEM] * 4 + [ANY] * len(ready),
                0,
                2**20,
                name="join",
                vmem=4,
            )(*pieces, *ready)
        )
    y2 = [swap(t, "xl") for t in y0]
    *y0, us[1], us[2], us[3] = lax.optimization_barrier((*y0, *us[1:]))
    split = []
    for t in us:
        t = t.astype(f32) * (1.0 / U_SCALE)
        high = lax.reduce_precision(t, 8, 7)
        split += [high.astype(bf16), (t - high).astype(bf16)]
    y1 = [swap(t, "c") for t in y0]
    y2[1], *split = lax.optimization_barrier((y2[1], *split))
    y3 = [swap(t, "c") for t in y2]

    return call(
        combine,
        (shape((ROWS, BLOCK), f32),) * 2,
        [SMEM] + [VMEM] * 19,
        8 * ROWS * DEPTH * BLOCK,
        8 * 2**20,
        [pltpu.VMEM((2, ROWS, DEPTH), bf16)],
        name="combine",
        vmem=20,
    )(place, sums, pa, pb, *y0, *y1, *y2, *y3, *split)


def solution(mesh):
    fine = Mesh(np.asarray(mesh.devices).reshape(tuple(PARTS.values())), tuple(PARTS))
    return jax.shard_map(
        local,
        mesh=fine,
        in_specs=(P(DP, None), P(DP, None), P(None, FEAT)),
        out_specs=(P(DP, FEAT), P(DP, FEAT)),
        check_vma=False,
    )
```

```python
import jax
import jax.numpy as jnp
import numpy as np
from jax import lax
from jax.experimental import pallas as pl
from jax.experimental.pallas import tpu as pltpu
from jax.sharding import Mesh, PartitionSpec as P

DP = ("xh", "y")
FEAT = ("z", "xl", "c")
PARTS = {"xh": 2, "y": 4, "z": 8, "xl": 2, "c": 2}
SWAP = [(0, 1), (1, 0)]
U_SCALE = 1024.0
EPS = 1e-05
f32, bf16, f16 = jnp.float32, jnp.bfloat16, jnp.float16

ROWS = 384
TOTAL = 3072
DEPTH = 1536
BLOCK = 256
QUARTER = ROWS // 4
PIECE = (48, 768)
SHARE = DEPTH // 4
VMEM = pl.BlockSpec(memory_space=pltpu.VMEM)
SMEM = pl.BlockSpec(memory_space=pltpu.SMEM)
ANY = pl.BlockSpec(memory_space=pl.ANY)


def exchange(blocks, axes):
    return lax.all_to_all(blocks, axes, split_axis=0, concat_axis=0, tiled=True)


def dot(a, b, ca, cb):
    return lax.dot_general(a, b, (((ca,), (cb,)), ((), ())), preferred_element_type=f32)


def call(body, out, ins, flops, nbytes, scratch=(), name=None, out_specs=None, vmem=60):
    return pl.pallas_call(
        body,
        out_shape=out,
        in_specs=ins,
        out_specs=out_specs or jax.tree.map(lambda _: VMEM, out),
        scratch_shapes=scratch,
        compiler_params=pltpu.CompilerParams(vmem_limit_bytes=vmem * 2**20),
        cost_estimate=pl.CostEstimate(flops=flops, bytes_accessed=nbytes, transcendentals=0),
        name=name,
    )


def project(va, vb, w, pa, pb, sums, xa, xb, xw, sem):
    third = DEPTH // 3
    copies = []
    for k in range(3):
        at = pl.ds(k * third, third)
        copies.append(
            [
                pltpu.make_async_copy(va.at[:, at], xa.at[k], sem.at[3 * k]),
                pltpu.make_async_copy(vb.at[:, at], xb.at[k], sem.at[3 * k + 1]),
                pltpu.make_async_copy(w.at[at, :], xw.at[k], sem.at[3 * k + 2]),
            ]
        )
    for c in copies:
        for t in c:
            t.start()
    a = b = 0.0
    for k in range(3):
        for t in copies[k]:
            t.wait()
        a = a + dot(xa[k], xw[k], 1, 0)
        b = b + dot(xb[k], xw[k], 1, 0)
    pa[...] = a
    pb[...] = b
    col = [jnp.sum(t, axis=0, keepdims=True) for t in (a, a * a, b, b * b, a * b)]
    own = jnp.concatenate(col + [jnp.zeros((3, BLOCK), f32)], axis=0)
    sums[...] = jnp.broadcast_to(own[None], sums.shape)


def moments(sums, q):
    t = sums[q]
    for d in range(1, 8):
        t = t + sums[4 * d + q]
    t = t * (1.0 / TOTAL)
    ma, mb = t[0:1], t[2:3]
    ra = lax.rsqrt(t[1:2] - ma * ma + EPS)
    rb = lax.rsqrt(t[3:4] - mb * mb + EPS)
    return ma, ra, mb, rb, (t[4:5] - ma * mb) * ra * rb


def embed(place, sums, v, w0, w1, w2, w3, y, na, nb):
    q = place[0]
    ws = (w0, w1, w2, w3)
    for j, wj in enumerate(ws):
        ma, ra, mb, rb, _ = moments(sums, q ^ j)
        p = dot(v[...], wj[...], 1, 0)
        cols = slice(j * BLOCK, (j + 1) * BLOCK)
        na[:, cols] = ((p[:QUARTER] - ma) * (ra * ra)).astype(bf16)
        nb[:, cols] = ((p[QUARTER:] - mb) * (rb * rb)).astype(bf16)
    n = jnp.concatenate([na[...], nb[...]], axis=0)
    for k in range(6):
        acc = 0.0
        for j, wj in enumerate(ws):
            nj = n[:, j * BLOCK : (j + 1) * BLOCK]
            acc = acc + dot(nj, wj[k * 256 : (k + 1) * 256, :], 1, 1)
        acc = acc.astype(bf16)
        for i in range(4):
            y[2 * i + k // 3, :, (k % 3) * 256 : (k % 3 + 1) * 256] = acc[48 * i : 48 * i + 48]


def add_copies(parts, ready, out):
    total = parts[0].astype(f32)
    for d in range(1, 8):
        total = total + parts[d].astype(f32)
    out[...] = jnp.broadcast_to(total.astype(bf16)[None], out.shape)


def turn(place, va, vb, ta, tb, quarter):
    at = pl.ds(pl.multiple_of(place[0] * QUARTER, 32), QUARTER)
    quarter[:QUARTER] = va[at, :]
    quarter[QUARTER:] = vb[at, :]
    for view, out in ((va, ta), (vb, tb)):
        v = view[...]
        centre = jnp.sum(v.astype(f32), axis=0, keepdims=True) * (1.0 / ROWS)
        centre = jnp.concatenate([centre, jnp.zeros((15, DEPTH), f32)], axis=0).astype(bf16)
        out[...] = jnp.concatenate([v, centre, jnp.zeros((112, DEPTH), bf16)], axis=0).T


def correlate(place, sums, pa, pb, ta, tb, ready, u0, u1, u2, u3, xs, xpa, xpb, xa, xb, x0, x1, x2, x3, sem, out_sem):
    q, yy = place[0], place[1]
    stats = [
        pltpu.make_async_copy(src, dst, sem.at[8 + i])
        for i, (src, dst) in enumerate(((sums, xs), (pa, xpa), (pb, xpb)))
    ]
    copies = {}
    for s in (1, 2, 3, 0):
        at = pl.ds(pl.multiple_of(((yy + s) & 3) * SHARE, SHARE), SHARE)
        copies[s] = (
            pltpu.make_async_copy(ta.at[at, :], xa.at[s], sem.at[2 * s]),
            pltpu.make_async_copy(tb.at[at, :], xb.at[s], sem.at[2 * s + 1]),
        )
    for t in stats:
        t.start()
    for c in copies.values():
        for t in c:
            t.start()
    for t in stats:
        t.wait()
    ma, ra, mb, rb, _ = moments(xs, q)
    ns = []
    for p, m, s in ((xpa, ma, ra), (xpb, mb, rb)):
        n = (p[...] - m) * s
        rounded = n.astype(bf16)
        excess = jnp.sum(n - rounded.astype(f32), axis=0, keepdims=True)
        excess = jnp.concatenate([excess, jnp.zeros((15, BLOCK), f32)], axis=0).astype(bf16)
        ns.append(jnp.concatenate([rounded, excess, jnp.zeros((112, BLOCK), bf16)], axis=0))
    scale = U_SCALE / TOTAL
    done = []
    for s, x, u in ((1, x1, u1), (2, x2, u2), (3, x3, u3), (0, x0, u0)):
        for t in copies[s]:
            t.wait()
        x[:, :BLOCK] = (dot(xb[s], ns[0], 1, 0) * scale).astype(x.dtype)
        x[:, BLOCK:] = (dot(xa[s], ns[1], 1, 0) * scale).astype(x.dtype)
        out = pltpu.make_async_copy(x, u, out_sem.at[s])
        out.start()
        done.append(out)
    for t in done:
        t.wait()


def combine(place, sums, pa, pb, *refs):
    ys, us, (out_a, out_b, ya, yb) = refs[:8], refs[8:16], refs[16:]
    q, yy = place[0], place[1]
    for j in range(4):
        for i in range(4):
            at = pl.multiple_of((q ^ j) * QUARTER + (i & 1) * 48, 16)
            for h in range(2):
                to = ya if i < 2 else yb
                to[pl.ds(at, 48), h * 768 : (h + 1) * 768] = ys[2 * j + i // 2][2 * (i & 1) + h]
    ma, ra, mb, rb, corr = moments(sums, q)
    for first, y, p, m, r, out in (
        (0, yb, pb, mb, rb, out_a),
        (BLOCK, ya, pa, ma, ra, out_b),
    ):
        acc = (p[...] - m) * (r * (corr - 2.0))
        cols = slice(first, first + BLOCK)
        for s in range(4):
            at = pl.ds(pl.multiple_of(((yy + 4 - s) & 3) * SHARE, 128), SHARE)
            part = y[:, at]
            acc = acc + (dot(part, us[2 * s][:, cols], 1, 0) + dot(part, us[2 * s + 1][:, cols], 1, 0))
        out[...] = acc


def mark(arrived, out):
    out[...] = jnp.zeros(out.shape, f32)


def arrival(t, us):
    return pl.pallas_call(
        mark,
        out_shape=jax.ShapeDtypeStruct((8, 128), f32),
        in_specs=[ANY],
        out_specs=VMEM,
        cost_estimate=pl.CostEstimate(flops=us * 10**9, bytes_accessed=0, transcendentals=0),
        name="mark",
    )(t)


def halve(whole, ready, first, second):
    first[...] = whole[:4]
    second[...] = whole[4:]


def local(va, vb, w):
    q = lax.axis_index("xl") * 2 + lax.axis_index("c")
    place = jnp.stack([q, lax.axis_index("y")]).astype(jnp.int32)
    shape = jax.ShapeDtypeStruct
    sems = pltpu.SemaphoreType.DMA

    def swap(t, axis):
        return lax.ppermute(t, axis, SWAP)

    def along_y(t, s):
        return lax.ppermute(t, "y", [(i, (i + s) % 4) for i in range(4)])

    w_x = swap(w, "xl")
    w_c = swap(w, "c")

    pa, pb, own = call(
        project,
        (shape((ROWS, BLOCK), f32), shape((ROWS, BLOCK), f32), shape((32, 8, BLOCK), f32)),
        [ANY] * 3,
        4 * ROWS * DEPTH * BLOCK,
        4 * 2**20,
        [
            pltpu.VMEM((3, ROWS, DEPTH // 3), bf16),
            pltpu.VMEM((3, ROWS, DEPTH // 3), bf16),
            pltpu.VMEM((3, DEPTH // 3, BLOCK), bf16),
            sems((9,)),
        ],
        name="project",
    )(va, vb, w)
    sums = exchange(own, ("xh", "y", "xl", "c"))
    va, vb, pa = lax.optimization_barrier((va, vb, pa))
    ta, tb, v_quarter = call(
        turn,
        (shape((DEPTH, 512), bf16),) * 2 + (shape((2 * QUARTER, DEPTH), bf16),),
        [SMEM] + [VMEM] * 2,
        10 * 2**20,
        6 * 2**20,
        name="turn",
    )(place, va, vb)
    sums, ta, tb, v_quarter, w_x = lax.optimization_barrier((sums, ta, tb, v_quarter, w_x))
    w_xc = swap(w_x, "c")

    y_part = call(
        embed,
        shape((8,) + PIECE, bf16),
        [SMEM] + [VMEM] * 6,
        16 * ROWS * DEPTH * BLOCK // 2,
        7 * 2**20,
        [pltpu.VMEM((QUARTER, 4 * BLOCK), bf16)] * 2,
        name="embed",
        vmem=20,
    )(place, sums, v_quarter, w, w_c, w_x, w_xc)
    y_parts = exchange(y_part, "z")

    u_parts = call(
        correlate,
        (shape((SHARE, 2 * BLOCK), f32),) + (shape((SHARE, 2 * BLOCK), bf16),) * 3,
        [SMEM] + [ANY] * 6,
        4 * ROWS * DEPTH * BLOCK,
        6 * 2**20,
        [
            pltpu.VMEM((32, 8, BLOCK), f32),
            pltpu.VMEM((ROWS, BLOCK), f32),
            pltpu.VMEM((ROWS, BLOCK), f32),
            pltpu.VMEM((4, SHARE, 512), bf16),
            pltpu.VMEM((4, SHARE, 512), bf16),
            pltpu.VMEM((SHARE, 2 * BLOCK), f32),
            pltpu.VMEM((SHARE, 2 * BLOCK), bf16),
            pltpu.VMEM((SHARE, 2 * BLOCK), bf16),
            pltpu.VMEM((SHARE, 2 * BLOCK), bf16),
            sems((11,)),
            sems((4,)),
        ],
        out_specs=(ANY,) * 4,
        name="correlate",
    )(place, sums, pa, pb, ta, tb, y_part)
    u = u_parts[0]
    for s in (1, 2, 3):
        u = u + along_y(u_parts[s], s).astype(f32)
    u_near = arrival(u[:8, :128], 2)
    u = u.astype(f16)
    u = u.astype(f32) + swap(u, "xh").astype(f32)
    u_far = arrival(u[:8, :128], 4)
    u = lax.optimization_barrier(u.astype(f16))
    us = [u] + [along_y(u, s) for s in (1, 2, 3)]

    y_copies = call(
        add_copies,
        shape((8,) + PIECE, bf16),
        [VMEM] * 2,
        10 * 2**20,
        2**20,
        name="add_copies",
        vmem=4,
    )(y_parts, u_near)
    y0 = call(
        halve,
        (shape((4,) + PIECE, bf16),) * 2,
        [VMEM] * 2,
        0,
        2**20,
        name="halve",
        vmem=4,
    )(exchange(y_copies, "z"), u_far)
    y2 = [swap(t, "xl") for t in y0]
    *y0, us[1], us[2], us[3] = lax.optimization_barrier((*y0, *us[1:]))
    split = []
    for t in us:
        t = t.astype(f32) * (1.0 / U_SCALE)
        high = lax.reduce_precision(t, 8, 7)
        split += [high.astype(bf16), (t - high).astype(bf16)]
    y1 = [swap(t, "c") for t in y0]
    y2[1], *split = lax.optimization_barrier((y2[1], *split))
    y3 = [swap(t, "c") for t in y2]

    return call(
        combine,
        (shape((ROWS, BLOCK), f32),) * 2,
        [SMEM] + [VMEM] * 19,
        8 * ROWS * DEPTH * BLOCK,
        8 * 2**20,
        [pltpu.VMEM((ROWS, DEPTH), bf16)] * 2,
        name="combine",
        vmem=20,
    )(place, sums, pa, pb, *y0, *y1, *y2, *y3, *split)


def solution(mesh):
    fine = Mesh(np.asarray(mesh.devices).reshape(tuple(PARTS.values())), tuple(PARTS))
    return jax.shard_map(
        local,
        mesh=fine,
        in_specs=(P(DP, None), P(DP, None), P(None, FEAT)),
        out_specs=(P(DP, FEAT), P(DP, FEAT)),
        check_vma=False,
    )
```

```python
import jax
import jax.numpy as jnp
import numpy as np
from jax import lax
from jax.experimental import pallas as pl
from jax.experimental.pallas import tpu as pltpu
from jax.sharding import Mesh, PartitionSpec as P

DP = ("xh", "y")
FEAT = ("z", "xl", "c")
PARTS = {"xh": 2, "y": 4, "z": 8, "xl": 2, "c": 2}
SWAP = [(0, 1), (1, 0)]
U_SCALE = 1024.0
EPS = 1e-05
f32, bf16, f16 = jnp.float32, jnp.bfloat16, jnp.float16

ROWS = 384
TOTAL = 3072
DEPTH = 1536
BLOCK = 256
QUARTER = ROWS // 4
PIECE = (48, 768)
SHARE = DEPTH // 4
VMEM = pl.BlockSpec(memory_space=pltpu.VMEM)
SMEM = pl.BlockSpec(memory_space=pltpu.SMEM)
ANY = pl.BlockSpec(memory_space=pl.ANY)


def exchange(blocks, axes):
    return lax.all_to_all(blocks, axes, split_axis=0, concat_axis=0, tiled=True)


def dot(a, b, ca, cb):
    return lax.dot_general(a, b, (((ca,), (cb,)), ((), ())), preferred_element_type=f32)


def call(body, out, ins, flops, nbytes, scratch=(), name=None, out_specs=None, vmem=60):
    return pl.pallas_call(
        body,
        out_shape=out,
        in_specs=ins,
        out_specs=out_specs or jax.tree.map(lambda _: VMEM, out),
        scratch_shapes=scratch,
        compiler_params=pltpu.CompilerParams(vmem_limit_bytes=vmem * 2**20),
        cost_estimate=pl.CostEstimate(flops=flops, bytes_accessed=nbytes, transcendentals=0),
        name=name,
    )


def project(va, vb, w, pa, pb, sums, xa, xb, xw, sem):
    third = DEPTH // 3
    copies = []
    for k in range(3):
        at = pl.ds(k * third, third)
        copies.append(
            [
                pltpu.make_async_copy(va.at[:, at], xa.at[k], sem.at[3 * k]),
                pltpu.make_async_copy(vb.at[:, at], xb.at[k], sem.at[3 * k + 1]),
                pltpu.make_async_copy(w.at[at, :], xw.at[k], sem.at[3 * k + 2]),
            ]
        )
    for c in copies:
        for t in c:
            t.start()
    a = b = 0.0
    for k in range(3):
        for t in copies[k]:
            t.wait()
        a = a + dot(xa[k], xw[k], 1, 0)
        b = b + dot(xb[k], xw[k], 1, 0)
    pa[...] = a
    pb[...] = b
    col = [jnp.sum(t, axis=0, keepdims=True) for t in (a, a * a, b, b * b, a * b)]
    own = jnp.concatenate(col + [jnp.zeros((3, BLOCK), f32)], axis=0)
    sums[...] = jnp.broadcast_to(own[None], sums.shape)


def moments(sums, q):
    t = sums[q]
    for d in range(1, 8):
        t = t + sums[4 * d + q]
    t = t * (1.0 / TOTAL)
    ma, mb = t[0:1], t[2:3]
    ra = lax.rsqrt(t[1:2] - ma * ma + EPS)
    rb = lax.rsqrt(t[3:4] - mb * mb + EPS)
    return ma, ra, mb, rb, (t[4:5] - ma * mb) * ra * rb


def embed(place, sums, v, w0, w1, w2, w3, ready, y, na, nb):
    q = place[0]
    ws = (w0, w1, w2, w3)
    for j, wj in enumerate(ws):
        ma, ra, mb, rb, _ = moments(sums, q ^ j)
        p = dot(v[...], wj[...], 1, 0)
        cols = slice(j * BLOCK, (j + 1) * BLOCK)
        na[:, cols] = ((p[:QUARTER] - ma) * (ra * ra)).astype(bf16)
        nb[:, cols] = ((p[QUARTER:] - mb) * (rb * rb)).astype(bf16)
    n = jnp.concatenate([na[...], nb[...]], axis=0)
    for k in range(6):
        acc = 0.0
        for j, wj in enumerate(ws):
            nj = n[:, j * BLOCK : (j + 1) * BLOCK]
            acc = acc + dot(nj, wj[k * 256 : (k + 1) * 256, :], 1, 1)
        acc = acc.astype(bf16)
        for i in range(4):
            y[2 * i + k // 3, :, (k % 3) * 256 : (k % 3 + 1) * 256] = acc[48 * i : 48 * i + 48]


def add_copies(parts, ready, out):
    total = parts[0].astype(f32)
    for d in range(1, 8):
        total = total + parts[d].astype(f32)
    out[...] = jnp.broadcast_to(total.astype(bf16)[None], out.shape)


def turn(place, va, vb, ta, tb, quarter):
    at = pl.ds(pl.multiple_of(place[0] * QUARTER, 32), QUARTER)
    quarter[:QUARTER] = va[at, :]
    quarter[QUARTER:] = vb[at, :]
    for view, out in ((va, ta), (vb, tb)):
        v = view[...]
        centre = jnp.sum(v.astype(f32), axis=0, keepdims=True) * (1.0 / ROWS)
        centre = jnp.concatenate([centre, jnp.zeros((15, DEPTH), f32)], axis=0).astype(bf16)
        out[...] = jnp.concatenate([v, centre, jnp.zeros((112, DEPTH), bf16)], axis=0).T


def correlate(place, sums, pa, pb, ta, tb, u0, u1, u2, u3, xs, xpa, xpb, xa, xb, x0, x1, x2, x3, sem, out_sem):
    q, yy = place[0], place[1]
    stats = [
        pltpu.make_async_copy(src, dst, sem.at[8 + i])
        for i, (src, dst) in enumerate(((sums, xs), (pa, xpa), (pb, xpb)))
    ]
    copies = {}
    for s in (1, 2, 3, 0):
        at = pl.ds(pl.multiple_of(((yy + s) & 3) * SHARE, SHARE), SHARE)
        copies[s] = (
            pltpu.make_async_copy(ta.at[at, :], xa.at[s], sem.at[2 * s]),
            pltpu.make_async_copy(tb.at[at, :], xb.at[s], sem.at[2 * s + 1]),
        )
    for t in stats:
        t.start()
    for c in copies.values():
        for t in c:
            t.start()
    for t in stats:
        t.wait()
    ma, ra, mb, rb, _ = moments(xs, q)
    ns = []
    for p, m, s in ((xpa, ma, ra), (xpb, mb, rb)):
        n = (p[...] - m) * s
        rounded = n.astype(bf16)
        excess = jnp.sum(n - rounded.astype(f32), axis=0, keepdims=True)
        excess = jnp.concatenate([excess, jnp.zeros((15, BLOCK), f32)], axis=0).astype(bf16)
        ns.append(jnp.concatenate([rounded, excess, jnp.zeros((112, BLOCK), bf16)], axis=0))
    scale = U_SCALE / TOTAL
    done = []
    for s, x, u in ((1, x1, u1), (2, x2, u2), (3, x3, u3), (0, x0, u0)):
        for t in copies[s]:
            t.wait()
        x[:, :BLOCK] = (dot(xb[s], ns[0], 1, 0) * scale).astype(x.dtype)
        x[:, BLOCK:] = (dot(xa[s], ns[1], 1, 0) * scale).astype(x.dtype)
        out = pltpu.make_async_copy(x, u, out_sem.at[s])
        out.start()
        done.append(out)
    for t in done:
        t.wait()


def combine(place, sums, pa, pb, *refs):
    ys, us, (out_a, out_b, ya, yb) = refs[:8], refs[8:16], refs[16:]
    q, yy = place[0], place[1]
    for j in range(4):
        for i in range(4):
            at = pl.multiple_of((q ^ j) * QUARTER + (i & 1) * 48, 16)
            for h in range(2):
                to = ya if i < 2 else yb
                to[pl.ds(at, 48), h * 768 : (h + 1) * 768] = ys[2 * j + i // 2][2 * (i & 1) + h]
    ma, ra, mb, rb, corr = moments(sums, q)
    for first, y, p, m, r, out in (
        (0, yb, pb, mb, rb, out_a),
        (BLOCK, ya, pa, ma, ra, out_b),
    ):
        acc = (p[...] - m) * (r * (corr - 2.0))
        cols = slice(first, first + BLOCK)
        for s in range(4):
            at = pl.ds(pl.multiple_of(((yy + 4 - s) & 3) * SHARE, 128), SHARE)
            part = y[:, at]
            acc = acc + (dot(part, us[2 * s][:, cols], 1, 0) + dot(part, us[2 * s + 1][:, cols], 1, 0))
        out[...] = acc


def mark(arrived, out):
    out[...] = jnp.zeros(out.shape, f32)


def arrival(t, us):
    return pl.pallas_call(
        mark,
        out_shape=jax.ShapeDtypeStruct((8, 128), f32),
        in_specs=[ANY],
        out_specs=VMEM,
        cost_estimate=pl.CostEstimate(flops=us * 10**9, bytes_accessed=0, transcendentals=0),
        name="mark",
    )(t)


def halve(whole, ready, first, second):
    first[...] = whole[:4]
    second[...] = whole[4:]


def local(va, vb, w):
    q = lax.axis_index("xl") * 2 + lax.axis_index("c")
    place = jnp.stack([q, lax.axis_index("y")]).astype(jnp.int32)
    shape = jax.ShapeDtypeStruct
    sems = pltpu.SemaphoreType.DMA

    def swap(t, axis):
        return lax.ppermute(t, axis, SWAP)

    def along_y(t, s):
        return lax.ppermute(t, "y", [(i, (i + s) % 4) for i in range(4)])

    w_x = swap(w, "xl")
    w_c = swap(w, "c")

    pa, pb, own = call(
        project,
        (shape((ROWS, BLOCK), f32), shape((ROWS, BLOCK), f32), shape((32, 8, BLOCK), f32)),
        [ANY] * 3,
        4 * ROWS * DEPTH * BLOCK,
        4 * 2**20,
        [
            pltpu.VMEM((3, ROWS, DEPTH // 3), bf16),
            pltpu.VMEM((3, ROWS, DEPTH // 3), bf16),
            pltpu.VMEM((3, DEPTH // 3, BLOCK), bf16),
            sems((9,)),
        ],
        name="project",
    )(va, vb, w)
    sums = exchange(own, ("xh", "y", "xl", "c"))
    va, vb, pa = lax.optimization_barrier((va, vb, pa))
    ta, tb, v_quarter = call(
        turn,
        (shape((DEPTH, 512), bf16),) * 2 + (shape((2 * QUARTER, DEPTH), bf16),),
        [SMEM] + [VMEM] * 2,
        10 * 2**20,
        6 * 2**20,
        name="turn",
    )(place, va, vb)
    sums, ta, tb, v_quarter, w_x = lax.optimization_barrier((sums, ta, tb, v_quarter, w_x))
    w_xc = swap(w_x, "c")

    u_parts = call(
        correlate,
        (shape((SHARE, 2 * BLOCK), f32),) + (shape((SHARE, 2 * BLOCK), bf16),) * 3,
        [SMEM] + [ANY] * 5,
        4 * ROWS * DEPTH * BLOCK,
        6 * 2**20,
        [
            pltpu.VMEM((32, 8, BLOCK), f32),
            pltpu.VMEM((ROWS, BLOCK), f32),
            pltpu.VMEM((ROWS, BLOCK), f32),
            pltpu.VMEM((4, SHARE, 512), bf16),
            pltpu.VMEM((4, SHARE, 512), bf16),
            pltpu.VMEM((SHARE, 2 * BLOCK), f32),
            pltpu.VMEM((SHARE, 2 * BLOCK), bf16),
            pltpu.VMEM((SHARE, 2 * BLOCK), bf16),
            pltpu.VMEM((SHARE, 2 * BLOCK), bf16),
            sems((11,)),
            sems((4,)),
        ],
        out_specs=(ANY,) * 4,
        name="correlate",
    )(place, sums, pa, pb, ta, tb)
    y_part = call(
        embed,
        shape((8,) + PIECE, bf16),
        [SMEM] + [VMEM] * 6 + [ANY],
        16 * ROWS * DEPTH * BLOCK // 2,
        7 * 2**20,
        [pltpu.VMEM((QUARTER, 4 * BLOCK), bf16)] * 2,
        name="embed",
        vmem=20,
    )(place, sums, v_quarter, w, w_c, w_x, w_xc, u_parts[0])
    y_parts = exchange(y_part, "z")

    u = u_parts[0]
    for s in (1, 2, 3):
        u = u + along_y(u_parts[s], s).astype(f32)
    u_near = arrival(u[:8, :128], 2)
    u = u.astype(f16)
    u = u.astype(f32) + swap(u, "xh").astype(f32)
    u_far = arrival(u[:8, :128], 4)
    u = lax.optimization_barrier(u.astype(f16))
    us = [u] + [along_y(u, s) for s in (1, 2, 3)]

    y_copies = call(
        add_copies,
        shape((8,) + PIECE, bf16),
        [VMEM] * 2,
        10 * 2**20,
        2**20,
        name="add_copies",
        vmem=4,
    )(y_parts, u_near)
    y0 = call(
        halve,
        (shape((4,) + PIECE, bf16),) * 2,
        [VMEM] * 2,
        0,
        2**20,
        name="halve",
        vmem=4,
    )(exchange(y_copies, "z"), u_far)
    y2 = [swap(t, "xl") for t in y0]
    *y0, us[1], us[2], us[3] = lax.optimization_barrier((*y0, *us[1:]))
    split = []
    for t in us:
        t = t.astype(f32) * (1.0 / U_SCALE)
        high = lax.reduce_precision(t, 8, 7)
        split += [high.astype(bf16), (t - high).astype(bf16)]
    y1 = [swap(t, "c") for t in y0]
    y2[1], *split = lax.optimization_barrier((y2[1], *split))
    y3 = [swap(t, "c") for t in y2]

    return call(
        combine,
        (shape((ROWS, BLOCK), f32),) * 2,
        [SMEM] + [VMEM] * 19,
        8 * ROWS * DEPTH * BLOCK,
        8 * 2**20,
        [pltpu.VMEM((ROWS, DEPTH), bf16)] * 2,
        name="combine",
        vmem=20,
    )(place, sums, pa, pb, *y0, *y1, *y2, *y3, *split)


def solution(mesh):
    fine = Mesh(np.asarray(mesh.devices).reshape(tuple(PARTS.values())), tuple(PARTS))
    return jax.shard_map(
        local,
        mesh=fine,
        in_specs=(P(DP, None), P(DP, None), P(None, FEAT)),
        out_specs=(P(DP, FEAT), P(DP, FEAT)),
        check_vma=False,
    )
```

```python
import jax
import jax.numpy as jnp
import numpy as np
from jax import lax
from jax.experimental import pallas as pl
from jax.experimental.pallas import tpu as pltpu
from jax.sharding import Mesh, PartitionSpec as P

DP = ("xh", "y")
FEAT = ("z", "xl", "c")
PARTS = {"xh": 2, "y": 4, "z": 8, "xl": 2, "c": 2}
SWAP = [(0, 1), (1, 0)]
U_SCALE = 1024.0
EPS = 1e-05
f32, bf16, f16 = jnp.float32, jnp.bfloat16, jnp.float16

ROWS = 384
TOTAL = 3072
DEPTH = 1536
BLOCK = 256
QUARTER = ROWS // 4
PIECE = (48, 768)
SHARE = DEPTH // 4
EARLY = 1024
VMEM = pl.BlockSpec(memory_space=pltpu.VMEM)
SMEM = pl.BlockSpec(memory_space=pltpu.SMEM)
ANY = pl.BlockSpec(memory_space=pl.ANY)


def exchange(blocks, axes):
    return lax.all_to_all(blocks, axes, split_axis=0, concat_axis=0, tiled=True)


def dot(a, b, ca, cb):
    return lax.dot_general(a, b, (((ca,), (cb,)), ((), ())), preferred_element_type=f32)


def call(body, out, ins, flops, nbytes, scratch=(), name=None, out_specs=None, vmem=60):
    return pl.pallas_call(
        body,
        out_shape=out,
        in_specs=ins,
        out_specs=out_specs or jax.tree.map(lambda _: VMEM, out),
        scratch_shapes=scratch,
        compiler_params=pltpu.CompilerParams(vmem_limit_bytes=vmem * 2**20),
        cost_estimate=pl.CostEstimate(flops=flops, bytes_accessed=nbytes, transcendentals=0),
        name=name,
    )


def project(va, vb, w, pa, pb, sums, xa, xb, xw, sem):
    third = DEPTH // 3
    copies = []
    for k in range(3):
        at = pl.ds(k * third, third)
        copies.append(
            [
                pltpu.make_async_copy(va.at[:, at], xa.at[k], sem.at[3 * k]),
                pltpu.make_async_copy(vb.at[:, at], xb.at[k], sem.at[3 * k + 1]),
                pltpu.make_async_copy(w.at[at, :], xw.at[k], sem.at[3 * k + 2]),
            ]
        )
    for c in copies:
        for t in c:
            t.start()
    a = b = 0.0
    for k in range(3):
        for t in copies[k]:
            t.wait()
        a = a + dot(xa[k], xw[k], 1, 0)
        b = b + dot(xb[k], xw[k], 1, 0)
    pa[...] = a
    pb[...] = b
    col = [jnp.sum(t, axis=0, keepdims=True) for t in (a, a * a, b, b * b, a * b)]
    own = jnp.concatenate(col + [jnp.zeros((3, BLOCK), f32)], axis=0)
    sums[...] = jnp.broadcast_to(own[None], sums.shape)


def moments(sums, q):
    t = sums[q]
    for d in range(1, 8):
        t = t + sums[4 * d + q]
    t = t * (1.0 / TOTAL)
    ma, mb = t[0:1], t[2:3]
    ra = lax.rsqrt(t[1:2] - ma * ma + EPS)
    rb = lax.rsqrt(t[3:4] - mb * mb + EPS)
    return ma, ra, mb, rb, (t[4:5] - ma * mb) * ra * rb


def embed(place, sums, v, w0, w1, w2, w2b, w3, w3b, y, na, nb):
    q = place[0]
    half = EARLY
    ws = ((w0,), (w1,), (w2, w2b), (w3, w3b))
    for j, wj in enumerate(ws):
        ma, ra, mb, rb, _ = moments(sums, q ^ j)
        if len(wj) == 1:
            p = dot(v[...], wj[0][...], 1, 0)
        else:
            p = dot(v[:, :half], wj[0][...], 1, 0) + dot(v[:, half:], wj[1][...], 1, 0)
        cols = slice(j * BLOCK, (j + 1) * BLOCK)
        na[:, cols] = ((p[:QUARTER] - ma) * (ra * ra)).astype(bf16)
        nb[:, cols] = ((p[QUARTER:] - mb) * (rb * rb)).astype(bf16)
    n = jnp.concatenate([na[...], nb[...]], axis=0)
    for k in range(6):
        acc = 0.0
        for j, wj in enumerate(ws):
            late = len(wj) == 2 and k * 256 >= EARLY
            part = wj[1] if late else wj[0]
            first = k * 256 - (EARLY if late else 0)
            nj = n[:, j * BLOCK : (j + 1) * BLOCK]
            acc = acc + dot(nj, part[first : first + 256, :], 1, 1)
        acc = acc.astype(bf16)
        for i in range(4):
            y[2 * i + k // 3, :, (k % 3) * 256 : (k % 3 + 1) * 256] = acc[48 * i : 48 * i + 48]


def add_copies(parts, ready, out):
    total = parts[0].astype(f32)
    for d in range(1, 8):
        total = total + parts[d].astype(f32)
    out[...] = jnp.broadcast_to(total.astype(bf16)[None], out.shape)


def turn(place, va, vb, ta, tb, quarter):
    at = pl.ds(pl.multiple_of(place[0] * QUARTER, 32), QUARTER)
    quarter[:QUARTER] = va[at, :]
    quarter[QUARTER:] = vb[at, :]
    for view, out in ((va, ta), (vb, tb)):
        v = view[...]
        centre = jnp.sum(v.astype(f32), axis=0, keepdims=True) * (1.0 / ROWS)
        centre = jnp.concatenate([centre, jnp.zeros((15, DEPTH), f32)], axis=0).astype(bf16)
        out[...] = jnp.concatenate([v, centre, jnp.zeros((112, DEPTH), bf16)], axis=0).T


def correlate(place, sums, pa, pb, ta, tb, u0, u1, u2, u3, xs, xpa, xpb, xa, xb, x0, x1, x2, x3, sem, out_sem):
    q, yy = place[0], place[1]
    stats = [
        pltpu.make_async_copy(src, dst, sem.at[8 + i])
        for i, (src, dst) in enumerate(((sums, xs), (pa, xpa), (pb, xpb)))
    ]
    copies = {}
    for s in (1, 2, 3, 0):
        at = pl.ds(pl.multiple_of(((yy + s) & 3) * SHARE, SHARE), SHARE)
        copies[s] = (
            pltpu.make_async_copy(ta.at[at, :], xa.at[s], sem.at[2 * s]),
            pltpu.make_async_copy(tb.at[at, :], xb.at[s], sem.at[2 * s + 1]),
        )
    for t in stats:
        t.start()
    for c in copies.values():
        for t in c:
            t.start()
    for t in stats:
        t.wait()
    ma, ra, mb, rb, _ = moments(xs, q)
    ns = []
    for p, m, s in ((xpa, ma, ra), (xpb, mb, rb)):
        n = (p[...] - m) * s
        rounded = n.astype(bf16)
        excess = jnp.sum(n - rounded.astype(f32), axis=0, keepdims=True)
        excess = jnp.concatenate([excess, jnp.zeros((15, BLOCK), f32)], axis=0).astype(bf16)
        ns.append(jnp.concatenate([rounded, excess, jnp.zeros((112, BLOCK), bf16)], axis=0))
    scale = U_SCALE / TOTAL
    done = []
    for s, x, u in ((1, x1, u1), (2, x2, u2), (3, x3, u3), (0, x0, u0)):
        for t in copies[s]:
            t.wait()
        x[:, :BLOCK] = (dot(xb[s], ns[0], 1, 0) * scale).astype(x.dtype)
        x[:, BLOCK:] = (dot(xa[s], ns[1], 1, 0) * scale).astype(x.dtype)
        out = pltpu.make_async_copy(x, u, out_sem.at[s])
        out.start()
        done.append(out)
    for t in done:
        t.wait()


def combine(place, sums, pa, pb, *refs):
    ys, us, (out_a, out_b, ya, yb) = refs[:8], refs[8:16], refs[16:]
    q, yy = place[0], place[1]
    for j in range(4):
        for i in range(4):
            at = pl.multiple_of((q ^ j) * QUARTER + (i & 1) * 48, 16)
            for h in range(2):
                to = ya if i < 2 else yb
                to[pl.ds(at, 48), h * 768 : (h + 1) * 768] = ys[2 * j + i // 2][2 * (i & 1) + h]
    ma, ra, mb, rb, corr = moments(sums, q)
    for first, y, p, m, r, out in (
        (0, yb, pb, mb, rb, out_a),
        (BLOCK, ya, pa, ma, ra, out_b),
    ):
        acc = (p[...] - m) * (r * (corr - 2.0))
        cols = slice(first, first + BLOCK)
        for s in range(4):
            at = pl.ds(pl.multiple_of(((yy + 4 - s) & 3) * SHARE, 128), SHARE)
            part = y[:, at]
            acc = acc + (dot(part, us[2 * s][:, cols], 1, 0) + dot(part, us[2 * s + 1][:, cols], 1, 0))
        out[...] = acc


def mark(arrived, out):
    out[...] = jnp.zeros(out.shape, f32)


def arrival(t, us):
    return pl.pallas_call(
        mark,
        out_shape=jax.ShapeDtypeStruct((8, 128), f32),
        in_specs=[ANY],
        out_specs=VMEM,
        compiler_params=pltpu.CompilerParams(vmem_limit_bytes=4 * 2**20),
        cost_estimate=pl.CostEstimate(flops=us * 10**9, bytes_accessed=0, transcendentals=0),
        name="mark",
    )(t)


def halve(whole, ready, first, second):
    first[...] = whole[:4]
    second[...] = whole[4:]


def local(va, vb, w):
    q = lax.axis_index("xl") * 2 + lax.axis_index("c")
    place = jnp.stack([q, lax.axis_index("y")]).astype(jnp.int32)
    shape = jax.ShapeDtypeStruct
    sems = pltpu.SemaphoreType.DMA
    half = EARLY

    def swap(t, axis):
        return lax.ppermute(t, axis, SWAP)

    def along_y(t, s):
        return lax.ppermute(t, "y", [(i, (i + s) % 4) for i in range(4)])

    w_c = swap(w, "c")
    w_x = swap(w[:half], "xl")

    pa, pb, own = call(
        project,
        (shape((ROWS, BLOCK), f32), shape((ROWS, BLOCK), f32), shape((32, 8, BLOCK), f32)),
        [ANY] * 3,
        4 * ROWS * DEPTH * BLOCK,
        4 * 2**20,
        [
            pltpu.VMEM((3, ROWS, DEPTH // 3), bf16),
            pltpu.VMEM((3, ROWS, DEPTH // 3), bf16),
            pltpu.VMEM((3, DEPTH // 3, BLOCK), bf16),
            sems((9,)),
        ],
        name="project",
    )(va, vb, w)
    sums = exchange(own, ("xh", "y", "xl", "c"))
    va, vb, pa = lax.optimization_barrier((va, vb, pa))
    ta, tb, v_quarter = call(
        turn,
        (shape((DEPTH, 512), bf16),) * 2 + (shape((2 * QUARTER, DEPTH), bf16),),
        [SMEM] + [VMEM] * 2,
        10 * 2**20,
        6 * 2**20,
        name="turn",
    )(place, va, vb)
    sums, ta, tb, v_quarter, w_late, w_x = lax.optimization_barrier(
        (sums, ta, tb, v_quarter, w[half:], w_x)
    )
    w_xb = swap(w_late, "xl")
    w_xcb = swap(w_xb, "c")

    u_parts = call(
        correlate,
        (shape((SHARE, 2 * BLOCK), f32),) + (shape((SHARE, 2 * BLOCK), bf16),) * 3,
        [SMEM] + [ANY] * 5,
        4 * ROWS * DEPTH * BLOCK,
        6 * 2**20,
        [
            pltpu.VMEM((32, 8, BLOCK), f32),
            pltpu.VMEM((ROWS, BLOCK), f32),
            pltpu.VMEM((ROWS, BLOCK), f32),
            pltpu.VMEM((4, SHARE, 512), bf16),
            pltpu.VMEM((4, SHARE, 512), bf16),
            pltpu.VMEM((SHARE, 2 * BLOCK), f32),
            pltpu.VMEM((SHARE, 2 * BLOCK), bf16),
            pltpu.VMEM((SHARE, 2 * BLOCK), bf16),
            pltpu.VMEM((SHARE, 2 * BLOCK), bf16),
            sems((11,)),
            sems((4,)),
        ],
        out_specs=(ANY,) * 4,
        name="correlate",
    )(place, sums, pa, pb, ta, tb)
    *u_parts, w_x = lax.optimization_barrier((*u_parts, w_x))
    w_xc = swap(w_x, "c")
    u = u_parts[0]
    for s in (1, 2, 3):
        u = u + along_y(u_parts[s], s).astype(f32)
    u_near = arrival(u[:8, :128], 8)
    u = u.astype(f16)
    u = u.astype(f32) + swap(u, "xh").astype(f32)
    u_far = arrival(u[:8, :128], 4)
    u = lax.optimization_barrier(u.astype(f16))
    us = [u] + [along_y(u, s) for s in (1, 2, 3)]

    y_part = call(
        embed,
        shape((8,) + PIECE, bf16),
        [SMEM] + [VMEM] * 8,
        16 * ROWS * DEPTH * BLOCK // 2,
        7 * 2**20,
        [pltpu.VMEM((QUARTER, 4 * BLOCK), bf16)] * 2,
        name="embed",
        vmem=20,
    )(place, sums, v_quarter, w, w_c, w_x, w_xb, w_xc, w_xcb)
    y_copies = call(
        add_copies,
        shape((8,) + PIECE, bf16),
        [VMEM] * 2,
        10 * 2**20,
        2**20,
        name="add_copies",
        vmem=4,
    )(exchange(y_part, "z"), u_near)
    y0 = call(
        halve,
        (shape((4,) + PIECE, bf16),) * 2,
        [VMEM] * 2,
        0,
        2**20,
        name="halve",
        vmem=4,
    )(exchange(y_copies, "z"), u_far)
    y2 = [swap(t, "xl") for t in y0]
    *y0, us[1], us[2], us[3] = lax.optimization_barrier((*y0, *us[1:]))
    split = []
    for t in us:
        t = t.astype(f32) * (1.0 / U_SCALE)
        high = lax.reduce_precision(t, 8, 7)
        split += [high.astype(bf16), (t - high).astype(bf16)]
    y1 = [swap(t, "c") for t in y0]
    y2[1], *split = lax.optimization_barrier((y2[1], *split))
    y3 = [swap(t, "c") for t in y2]

    return call(
        combine,
        (shape((ROWS, BLOCK), f32),) * 2,
        [SMEM] + [VMEM] * 19,
        8 * ROWS * DEPTH * BLOCK,
        8 * 2**20,
        [pltpu.VMEM((ROWS, DEPTH), bf16)] * 2,
        name="combine",
        vmem=20,
    )(place, sums, pa, pb, *y0, *y1, *y2, *y3, *split)


def solution(mesh):
    fine = Mesh(np.asarray(mesh.devices).reshape(tuple(PARTS.values())), tuple(PARTS))
    return jax.shard_map(
        local,
        mesh=fine,
        in_specs=(P(DP, None), P(DP, None), P(None, FEAT)),
        out_specs=(P(DP, FEAT), P(DP, FEAT)),
        check_vma=False,
    )
```

```python
import jax
import jax.numpy as jnp
import numpy as np
from jax import lax
from jax.experimental import pallas as pl
from jax.experimental.pallas import tpu as pltpu
from jax.sharding import Mesh, PartitionSpec as P

DP = ("xh", "y")
FEAT = ("z", "xl", "c")
PARTS = {"xh": 2, "y": 4, "z": 8, "xl": 2, "c": 2}
SWAP = [(0, 1), (1, 0)]
U_SCALE = 1536.0
EPS = 1e-05
f32, bf16, f16 = jnp.float32, jnp.bfloat16, jnp.float16

ROWS = 384
TOTAL = 3072
DEPTH = 1536
BLOCK = 256
QUARTER = ROWS // 4
PIECE = (48, 768)
SHARE = DEPTH // 4
EARLY = 1024
VMEM = pl.BlockSpec(memory_space=pltpu.VMEM)
SMEM = pl.BlockSpec(memory_space=pltpu.SMEM)
ANY = pl.BlockSpec(memory_space=pl.ANY)


def exchange(blocks, axes):
    return lax.all_to_all(blocks, axes, split_axis=0, concat_axis=0, tiled=True)


def dot(a, b, ca, cb):
    return lax.dot_general(a, b, (((ca,), (cb,)), ((), ())), preferred_element_type=f32)


def call(body, out, ins, flops, nbytes, scratch=(), name=None, out_specs=None, vmem=60):
    return pl.pallas_call(
        body,
        out_shape=out,
        in_specs=ins,
        out_specs=out_specs or jax.tree.map(lambda _: VMEM, out),
        scratch_shapes=scratch,
        compiler_params=pltpu.CompilerParams(vmem_limit_bytes=vmem * 2**20),
        cost_estimate=pl.CostEstimate(flops=flops, bytes_accessed=nbytes, transcendentals=0),
        name=name,
    )


def project(va, vb, w, pa, pb, sums, xa, xb, xw, sem):
    third = DEPTH // 3
    copies = []
    for k in range(3):
        at = pl.ds(k * third, third)
        copies.append(
            [
                pltpu.make_async_copy(va.at[:, at], xa.at[k], sem.at[3 * k]),
                pltpu.make_async_copy(vb.at[:, at], xb.at[k], sem.at[3 * k + 1]),
                pltpu.make_async_copy(w.at[at, :], xw.at[k], sem.at[3 * k + 2]),
            ]
        )
    for c in copies:
        for t in c:
            t.start()
    a = b = 0.0
    for k in range(3):
        for t in copies[k]:
            t.wait()
        a = a + dot(xa[k], xw[k], 1, 0)
        b = b + dot(xb[k], xw[k], 1, 0)
    pa[...] = a
    pb[...] = b
    col = [jnp.sum(t, axis=0, keepdims=True) for t in (a, a * a, b, b * b, a * b)]
    own = jnp.concatenate(col + [jnp.zeros((3, BLOCK), f32)], axis=0)
    sums[...] = jnp.broadcast_to(own[None], sums.shape)


def moments(sums, q):
    t = sums[q]
    for d in range(1, 8):
        t = t + sums[4 * d + q]
    t = t * (1.0 / TOTAL)
    ma, mb = t[0:1], t[2:3]
    ra = lax.rsqrt(t[1:2] - ma * ma + EPS)
    rb = lax.rsqrt(t[3:4] - mb * mb + EPS)
    return ma, ra, mb, rb, (t[4:5] - ma * mb) * ra * rb


def embed(place, sums, v, w0, w1, w2, w2b, w3, w3b, y, na, nb):
    q = place[0]
    half = EARLY
    ws = ((w0,), (w1,), (w2, w2b), (w3, w3b))
    for j, wj in enumerate(ws):
        ma, ra, mb, rb, _ = moments(sums, q ^ j)
        if len(wj) == 1:
            p = dot(v[...], wj[0][...], 1, 0)
        else:
            p = dot(v[:, :half], wj[0][...], 1, 0) + dot(v[:, half:], wj[1][...], 1, 0)
        cols = slice(j * BLOCK, (j + 1) * BLOCK)
        na[:, cols] = ((p[:QUARTER] - ma) * (ra * ra)).astype(bf16)
        nb[:, cols] = ((p[QUARTER:] - mb) * (rb * rb)).astype(bf16)
    n = jnp.concatenate([na[...], nb[...]], axis=0)
    for k in range(6):
        acc = 0.0
        for j, wj in enumerate(ws):
            late = len(wj) == 2 and k * 256 >= EARLY
            part = wj[1] if late else wj[0]
            first = k * 256 - (EARLY if late else 0)
            nj = n[:, j * BLOCK : (j + 1) * BLOCK]
            acc = acc + dot(nj, part[first : first + 256, :], 1, 1)
        acc = acc.astype(bf16)
        for i in range(4):
            y[2 * i + k // 3, :, (k % 3) * 256 : (k % 3 + 1) * 256] = acc[48 * i : 48 * i + 48]


def add_copies(parts, ready, out):
    total = parts[0].astype(f32)
    for d in range(1, 8):
        total = total + parts[d].astype(f32)
    out[...] = jnp.broadcast_to(total.astype(bf16)[None], out.shape)


def turn(place, va, vb, ta, tb, quarter):
    at = pl.ds(pl.multiple_of(place[0] * QUARTER, 32), QUARTER)
    quarter[:QUARTER] = va[at, :]
    quarter[QUARTER:] = vb[at, :]
    for view, out in ((va, ta), (vb, tb)):
        v = view[...]
        centre = jnp.sum(v.astype(f32), axis=0, keepdims=True) * (1.0 / ROWS)
        centre = jnp.concatenate([centre, jnp.zeros((15, DEPTH), f32)], axis=0).astype(bf16)
        out[...] = jnp.concatenate([v, centre, jnp.zeros((112, DEPTH), bf16)], axis=0).T


def correlate(place, sums, pa, pb, ta, tb, u0, u1, u2, u3, xs, xpa, xpb, xa, xb, x0, x1, x2, x3, sem, out_sem):
    q, yy = place[0], place[1]
    stats = [
        pltpu.make_async_copy(src, dst, sem.at[8 + i])
        for i, (src, dst) in enumerate(((sums, xs), (pa, xpa), (pb, xpb)))
    ]
    copies = {}
    for s in range(4):
        at = pl.ds(pl.multiple_of(((yy + s) & 3) * SHARE, SHARE), SHARE)
        copies[s] = (
            pltpu.make_async_copy(ta.at[at, :], xa.at[s], sem.at[2 * s]),
            pltpu.make_async_copy(tb.at[at, :], xb.at[s], sem.at[2 * s + 1]),
        )
    for t in stats:
        t.start()
    for c in copies.values():
        for t in c:
            t.start()
    for t in stats:
        t.wait()
    ma, ra, mb, rb, _ = moments(xs, q)
    ns = []
    for p, m, s in ((xpa, ma, ra), (xpb, mb, rb)):
        n = (p[...] - m) * s
        rounded = n.astype(bf16)
        excess = jnp.sum(n - rounded.astype(f32), axis=0, keepdims=True)
        excess = jnp.concatenate([excess, jnp.zeros((15, BLOCK), f32)], axis=0).astype(bf16)
        n = jnp.concatenate([rounded, excess, jnp.zeros((112, BLOCK), bf16)], axis=0)
        ns.append(n * (U_SCALE / TOTAL))
    done = []
    for s, x, u in ((0, x0, u0), (1, x1, u1), (2, x2, u2), (3, x3, u3)):
        for t in copies[s]:
            t.wait()
        x[:, :BLOCK] = dot(xb[s], ns[0], 1, 0).astype(x.dtype)
        x[:, BLOCK:] = dot(xa[s], ns[1], 1, 0).astype(x.dtype)
        out = pltpu.make_async_copy(x, u, out_sem.at[s])
        out.start()
        done.append(out)
    for t in done:
        t.wait()


def combine(place, sums, pa, pb, *refs):
    ys, us, (out_a, out_b, ya, yb) = refs[:8], refs[8:16], refs[16:]
    q, yy = place[0], place[1]
    for j in range(4):
        for i in range(4):
            at = pl.multiple_of((q ^ j) * QUARTER + (i & 1) * 48, 16)
            for h in range(2):
                to = ya if i < 2 else yb
                to[pl.ds(at, 48), h * 768 : (h + 1) * 768] = ys[2 * j + i // 2][2 * (i & 1) + h]
    ma, ra, mb, rb, corr = moments(sums, q)
    for first, y, p, m, r, out in (
        (0, yb, pb, mb, rb, out_a),
        (BLOCK, ya, pa, ma, ra, out_b),
    ):
        acc = (p[...] - m) * (r * (corr - 2.0))
        cols = slice(first, first + BLOCK)
        for s in range(4):
            at = pl.ds(pl.multiple_of(((yy + 4 - s) & 3) * SHARE, 128), SHARE)
            part = y[:, at]
            acc = acc + (dot(part, us[2 * s][:, cols], 1, 0) + dot(part, us[2 * s + 1][:, cols], 1, 0))
        out[...] = acc


def mark(arrived, out):
    out[...] = jnp.zeros(out.shape, f32)


def arrival(t, us):
    return pl.pallas_call(
        mark,
        out_shape=jax.ShapeDtypeStruct((8, 128), f32),
        in_specs=[ANY],
        out_specs=VMEM,
        compiler_params=pltpu.CompilerParams(vmem_limit_bytes=4 * 2**20),
        cost_estimate=pl.CostEstimate(flops=us * 10**9, bytes_accessed=0, transcendentals=0),
        name="mark",
    )(t)


def halve(whole, ready, first, second):
    first[...] = whole[:4]
    second[...] = whole[4:]


def local(va, vb, w):
    q = lax.axis_index("xl") * 2 + lax.axis_index("c")
    place = jnp.stack([q, lax.axis_index("y")]).astype(jnp.int32)
    shape = jax.ShapeDtypeStruct
    sems = pltpu.SemaphoreType.DMA
    half = EARLY

    def swap(t, axis):
        return lax.ppermute(t, axis, SWAP)

    def along_y(t, s):
        return lax.ppermute(t, "y", [(i, (i + s) % 4) for i in range(4)])

    w_c = swap(w, "c")
    w_x = swap(w[:half], "xl")

    pa, pb, own = call(
        project,
        (shape((ROWS, BLOCK), f32), shape((ROWS, BLOCK), f32), shape((32, 8, BLOCK), f32)),
        [ANY] * 3,
        4 * ROWS * DEPTH * BLOCK,
        4 * 2**20,
        [
            pltpu.VMEM((3, ROWS, DEPTH // 3), bf16),
            pltpu.VMEM((3, ROWS, DEPTH // 3), bf16),
            pltpu.VMEM((3, DEPTH // 3, BLOCK), bf16),
            sems((9,)),
        ],
        name="project",
    )(va, vb, w)
    sums = exchange(own, ("xh", "y", "xl", "c"))
    va, vb, pa = lax.optimization_barrier((va, vb, pa))
    ta, tb, v_quarter = call(
        turn,
        (shape((DEPTH, 512), bf16),) * 2 + (shape((2 * QUARTER, DEPTH), bf16),),
        [SMEM] + [VMEM] * 2,
        10 * 2**20,
        6 * 2**20,
        name="turn",
    )(place, va, vb)
    sums, ta, tb, v_quarter, w_late, w_x = lax.optimization_barrier(
        (sums, ta, tb, v_quarter, w[half:], w_x)
    )
    w_xb = swap(w_late, "xl")
    w_xcb = swap(w_xb, "c")

    u_parts = call(
        correlate,
        (shape((SHARE, 2 * BLOCK), f32),) + (shape((SHARE, 2 * BLOCK), bf16),) * 3,
        [SMEM] + [ANY] * 5,
        4 * ROWS * DEPTH * BLOCK,
        6 * 2**20,
        [
            pltpu.VMEM((32, 8, BLOCK), f32),
            pltpu.VMEM((ROWS, BLOCK), f32),
            pltpu.VMEM((ROWS, BLOCK), f32),
            pltpu.VMEM((4, SHARE, 512), bf16),
            pltpu.VMEM((4, SHARE, 512), bf16),
            pltpu.VMEM((SHARE, 2 * BLOCK), f32),
            pltpu.VMEM((SHARE, 2 * BLOCK), bf16),
            pltpu.VMEM((SHARE, 2 * BLOCK), bf16),
            pltpu.VMEM((SHARE, 2 * BLOCK), bf16),
            sems((11,)),
            sems((4,)),
        ],
        out_specs=(ANY,) * 4,
        name="correlate",
    )(place, sums, pa, pb, ta, tb)
    *u_parts, w_x = lax.optimization_barrier((*u_parts, w_x))
    w_xc = swap(w_x, "c")
    u = u_parts[0]
    for s in (1, 2, 3):
        u = u + along_y(u_parts[s], s).astype(f32)
    u_near = arrival(u[:8, :128], 8)
    u = u.astype(f16)
    u = u.astype(f32) + swap(u, "xh").astype(f32)
    u_far = arrival(u[:8, :128], 4)
    u = lax.optimization_barrier(u.astype(f16))
    us = [u] + [along_y(u, s) for s in (1, 2, 3)]

    y_part = call(
        embed,
        shape((8,) + PIECE, bf16),
        [SMEM] + [VMEM] * 8,
        16 * ROWS * DEPTH * BLOCK // 2,
        7 * 2**20,
        [pltpu.VMEM((QUARTER, 4 * BLOCK), bf16)] * 2,
        name="embed",
        vmem=20,
    )(place, sums, v_quarter, w, w_c, w_x, w_xb, w_xc, w_xcb)
    y_copies = call(
        add_copies,
        shape((8,) + PIECE, bf16),
        [VMEM] * 2,
        10 * 2**20,
        2**20,
        name="add_copies",
        vmem=4,
    )(exchange(y_part, "z"), u_near)
    y0 = call(
        halve,
        (shape((4,) + PIECE, bf16),) * 2,
        [VMEM] * 2,
        0,
        2**20,
        name="halve",
        vmem=4,
    )(exchange(y_copies, "z"), u_far)
    y2 = [swap(t, "xl") for t in y0]
    *y0, us[1], us[2], us[3] = lax.optimization_barrier((*y0, *us[1:]))
    split = []
    for t in us:
        t = t.astype(f32) * (1.0 / U_SCALE)
        high = lax.reduce_precision(t, 8, 7)
        split += [high.astype(bf16), (t - high).astype(bf16)]
    y1 = [swap(t, "c") for t in y0]
    y2[1], *split = lax.optimization_barrier((y2[1], *split))
    y3 = [swap(t, "c") for t in y2]

    return call(
        combine,
        (shape((ROWS, BLOCK), f32),) * 2,
        [SMEM] + [VMEM] * 19,
        8 * ROWS * DEPTH * BLOCK,
        8 * 2**20,
        [pltpu.VMEM((ROWS, DEPTH), bf16)] * 2,
        name="combine",
        vmem=20,
    )(place, sums, pa, pb, *y0, *y1, *y2, *y3, *split)


def solution(mesh):
    fine = Mesh(np.asarray(mesh.devices).reshape(tuple(PARTS.values())), tuple(PARTS))
    return jax.shard_map(
        local,
        mesh=fine,
        in_specs=(P(DP, None), P(DP, None), P(None, FEAT)),
        out_specs=(P(DP, FEAT), P(DP, FEAT)),
        check_vma=False,
    )
```
